32 devices in a mesh: group: 2 (over y), expert: 4 (over z), context: 2 (over x), tensor: 2 (over core).
Axes of the slice: x: 2, y: 2, z: 4, core: 2. Of those that a mesh axis runs over, the one named last changes fastest.
Arguments:
- tokens: bfloat16 [2048, 4096], P(('group', 'expert', 'context', 'tensor')), parts along dimension 0, may hold values from -6 to 6
- expert_ids: int32 [2048, 1], P(('group', 'expert', 'context', 'tensor')), parts along dimension 0, may hold values from 0 to 15; in each aligned block of 64 rows (0 to 63, 64 to 127, ...) at most 5 rows name the same one
- route_weights: float32 [2048, 1], P(('group', 'expert', 'context', 'tensor')), parts along dimension 0, may hold values from 0.05 to 1
- gate_weight: bfloat16 [16, 4096, 1536], P('expert', None, ('context', 'tensor')), may hold values from -0.09375 to 0.09375
- up_weight: bfloat16 [16, 4096, 1536], P('expert', None, ('context', 'tensor')), may hold values from -0.09375 to 0.09375
- down_weight: bfloat16 [16, 1536, 4096], P('expert', None, ('context', 'tensor')), may hold values from -0.15625 to 0.15625
Outputs:
- combined: bfloat16 [2048, 4096], P(('group', 'expert', 'context', 'tensor')), parts along dimension 0
The draws below stay inside these ranges and needn't reach their ends.
There are 2 independent parts, one for each index of `group`. The reference program is written for one: setup_inputs(seed, part) draws one part's arguments, and reference() takes and returns one part's arrays. A program takes and returns all parts, laid end to end along the dimension named above; an argument that names none is the same for every part. Nothing has to cross between parts.
Inputs may be any that keep to these rules, and one draw needn't show every extreme that they name: `expert_ids`: each row names 1 different experts. Within the rows of one device (aligned blocks of 64 rows) no expert is named by more than 5 rows, and in every draw some expert is named by exactly 5 rows of some block.
All inputs are finite; a program needn't handle non-finite values.
Results may differ from the reference program's by a relative error of at most 0.0057.
Values may be sent and summed in bfloat16 or wider, within the bound.
No kernel may reach another device: no remote copies, remote signals or barrier semaphores. Data moves between devices by JAX's collectives and lax.ppermute only.
A program may use at most 128 MiB of HBM per device.

```python
import math
import jax
import jax.numpy as jnp
import numpy as np
from jax import lax

D = 4096
FF = 1536
CHOSEN = 1
TOK_DEV = 64
EXPERTS = 16
CAPACITY = 5
TOKENS = 1024


def levels(rng, extent, cuts, least, top_value):
    def one(dim, blocks):
        draws = jax.random.uniform(jax.random.fold_in(jax.random.fold_in(rng, 6), dim), (blocks,), jnp.float32, least / len(cuts), top_value / len(cuts))
        return jnp.repeat(jnp.exp(draws), extent[dim] // blocks).reshape((-1,) + (1,) * (len(extent) - dim - 1))

    gain = one(*cuts[0])
    for cut in cuts[1:]:
        gain = gain * one(*cut)
    return gain


def shared_out(key, own, number, rows, amount, top, reach, lean):
    ranking = jax.random.permutation(key, amount)
    packed, ordinary = load_shares(amount, rows * top, reach, lean, True), load_shares(amount, rows * top, reach, lean, False)
    places = jnp.arange(amount)

    def named(tallies, rotation):
        used = int((tallies > 0).sum())
        fixed = max(1, used // 4)
        moved = fixed + (places - fixed + rotation * (used - fixed)) % max(1, amount - fixed)
        return jnp.zeros((amount,), jnp.int32).at[ranking[jnp.where(places < fixed, places, moved)]].set(jnp.asarray(tallies, jnp.int32))

    tallies = jnp.where(number % 4 == 0, named(packed, number // 4), named(ordinary, number - number // 4 - 1))
    mixed = jax.random.permutation(jax.random.fold_in(own, 3), amount)
    donor, receiver = mixed[0:amount // 2 * 2:2], mixed[1:amount // 2 * 2:2]
    room = jnp.minimum(tallies[donor] - 1, reach - tallies[receiver]) // 2
    room = jnp.where((donor == ranking[0]) | (receiver == ranking[0]) | (tallies[receiver] == 0), 0, jnp.maximum(room, 0))
    moved = jax.random.randint(jax.random.fold_in(own, 4), (amount // 2,), 0, 1 << 20) % (room + 1)
    tallies = tallies.at[donor].add(-moved).at[receiver].add(moved)
    items = jnp.searchsorted(jnp.cumsum(tallies), jnp.arange(rows * top), side="right").astype(jnp.int32)
    listing = items.reshape(top, rows).T
    listing = listing[jax.random.permutation(jax.random.fold_in(own, 1), rows)]
    rotation = jax.random.randint(jax.random.fold_in(own, 2), (rows, 1), 0, top)
    return jnp.take_along_axis(listing, (jnp.arange(top)[None, :] + rotation) % top, axis=1)


def load_shares(number_of, total, reach, slope, full):
    weights = [(1 << 20) // math.isqrt(grade ** slope) + 1 for grade in range(1, number_of + 1)]
    largest = reach if full else min(reach, max(-(-total // number_of), total * weights[0] // sum(weights)))
    least = 1 if total - largest >= number_of - 1 else 0
    holding, rest = [largest] + [least] * (number_of - 1), total - largest - least * (number_of - 1)
    while rest > 0:
        candidates = [i for i in range(1, number_of) if holding[i] < largest] or [i for i in range(1, number_of) if holding[i] < reach]
        whole, budget = sum([weights[i] for i in candidates]), rest
        for i in candidates:
            more = min(reach - holding[i], max(1, budget * weights[i] // whole), rest)
            holding[i] = holding[i] + more
            rest = rest - more
    return np.array(holding)


def bell_draw(stream_key, extent, scale, limit, cuts=(), kind=jnp.bfloat16):
    values = scale * jax.random.normal(stream_key, extent, jnp.float32)
    if cuts:
        values = values * levels(stream_key, extent, cuts, -0.22, 0.18)
    return jnp.clip(values, -limit, limit).astype(kind)


def setup_inputs(seed: int = 0, part: int = 0) -> dict:
    seeds = jax.random.split(jax.random.key(seed), 7)
    part_splits = jax.random.split(jax.random.fold_in(seeds[6], part), 7)
    tokens = bell_draw(part_splits[0], (TOKENS, D), 1.0, 6.0, ((0, 16),))
    expert_ids_keys = jax.random.split(jax.random.fold_in(part_splits[1], 1), TOKENS // TOK_DEV)
    expert_ids_turns = jax.random.permutation(jax.random.fold_in(part_splits[1], 3), TOKENS // TOK_DEV)
    expert_ids = jax.vmap(lambda own, number: shared_out(jax.random.fold_in(part_splits[1], 2), own, number, TOK_DEV, EXPERTS, CHOSEN, CAPACITY, 2))(expert_ids_keys, expert_ids_turns).reshape((TOKENS, CHOSEN))
    route_weights = jnp.clip(jnp.exp(math.log(1.0) - 2.9957323 * jax.random.uniform(part_splits[2], (TOKENS, CHOSEN), jnp.float32) ** levels(part_splits[2], (TOKENS, CHOSEN), ((0, 16),), -0.2, 0.2)), 0.05, 1.0)
    gate_weight = bell_draw(seeds[3], (EXPERTS, D, FF), D ** -0.5, 0.09375, ((0, 4), (2, 4)))
    up_weight = bell_draw(seeds[4], (EXPERTS, D, FF), D ** -0.5, 0.09375, ((0, 4), (2, 4)))
    down_weight = bell_draw(seeds[5], (EXPERTS, FF, D), FF ** -0.5, 0.15625, ((0, 4), (2, 4)))
    return dict(tokens=tokens, expert_ids=expert_ids, route_weights=route_weights, gate_weight=gate_weight, up_weight=up_weight, down_weight=down_weight)


def reference(tokens, expert_ids, route_weights, gate_weight, up_weight, down_weight):
    blocks = TOKENS // TOK_DEV
    expert_table = jnp.arange(EXPERTS, dtype=jnp.int32)
    chosen = expert_ids[:, :, None] == expert_table[None, None, :]
    member = jnp.sum(chosen.astype(jnp.int32), axis=1).astype(jnp.int32)
    weight_of = jnp.sum(jnp.where(chosen, route_weights[:, :, None], jnp.zeros((), route_weights.dtype)), axis=1)
    running = jnp.cumsum(member.reshape(blocks, TOK_DEV, EXPERTS), axis=1).astype(jnp.int32)
    slot_rank = running.reshape(TOKENS, EXPERTS) - 1
    token_index = jnp.arange(TOKENS, dtype=jnp.int32)
    position = (token_index // TOK_DEV)[:, None] * CAPACITY + slot_rank
    position = jnp.where(member > 0, position, blocks * CAPACITY).astype(jnp.int32)
    expert_column = jnp.broadcast_to(expert_table[None, :], (TOKENS, EXPERTS))
    source_rows = jnp.broadcast_to(token_index[:, None], (TOKENS, EXPERTS))
    row_table = jnp.full((EXPERTS, blocks * CAPACITY), TOKENS, dtype=jnp.int32)
    row_table = row_table.at[expert_column, position].set(source_rows, mode="drop")
    padded = jnp.concatenate([tokens, jnp.zeros((1, D), tokens.dtype)], axis=0)
    weight_pad = jnp.concatenate([weight_of, jnp.zeros((1, EXPERTS), weight_of.dtype)], axis=0)
    weights_by_expert = weight_pad.T

    def one_expert(accumulated, inputs):
        gate_part, up_part, down_part, row_index, weight_row = inputs
        row_data = padded[row_index]
        gate_act = jnp.dot(row_data, gate_part, preferred_element_type=jnp.float32)
        upward = jnp.dot(row_data, up_part, preferred_element_type=jnp.float32)
        hidden = (jax.nn.silu(gate_act) * upward).astype(jnp.bfloat16)
        output = jnp.dot(hidden, down_part, preferred_element_type=jnp.float32).astype(jnp.bfloat16)
        scales = weight_row[row_index]
        accumulated = accumulated.at[row_index].add(scales[:, None] * output.astype(jnp.float32), mode="drop")
        return accumulated, None

    initial = jnp.zeros((TOKENS, D), jnp.float32)
    result, unused = lax.scan(one_expert, initial, (gate_weight, up_weight, down_weight, row_table, weights_by_expert))
    return result.astype(jnp.bfloat16)
```

```python
import functools
import jax
import jax.numpy as jnp
from jax import lax
from jax.experimental import pallas as pl
from jax.experimental.pallas import tpu as pltpu
from jax.sharding import PartitionSpec as P

BIG = 4096
PARTS = 2
VMEM_LIMIT = 48 * 1024 * 1024
F32, BF16, I32 = jnp.float32, jnp.bfloat16, jnp.int32


def div(x, by):
    return ((x.astype(F32) + 0.5) * (1.0 / by)).astype(I32)


def onehot(cond):
    return jnp.where(cond, 1.0, 0.0).astype(BF16)


def dot(a, b):
    return jnp.dot(a, b, preferred_element_type=F32)


def iota(shape, dim):
    return lax.broadcasted_iota(I32, shape, dim)


def as_column(row):
    n = row.shape[1]
    square = jnp.broadcast_to(row, (n, n))
    return jnp.sum(jnp.where(iota((n, n), 0) == iota((n, n), 1), square, jnp.zeros((), row.dtype)), axis=1, keepdims=True)


def slot_keys(ids_row, cap):
    n = ids_row.shape[1]
    ids_col = as_column(ids_row)
    earlier = (ids_col == ids_row) & (iota((n, n), 0) < iota((n, n), 1))
    rank = jnp.sum(jnp.where(earlier, 1, 0), axis=0, keepdims=True)
    return ids_row * cap + rank


def dispatch_kernel(cfg, pos_ref, ids_ref, tok_ref, *outs):
    z = pos_ref[0]
    n = tok_ref.shape[0]
    keys = slot_keys(ids_ref[...], cfg.cap)
    keys = jnp.concatenate([keys + j * BIG for j in range(cfg.nd)], axis=1)
    stacked = jnp.concatenate([tok_ref[:, j * cfg.w:(j + 1) * cfg.w] for j in range(cfg.nd)], axis=0)
    i = iota((cfg.rp, 1), 0)
    j = div(i, cfg.rows)
    target = i - j * cfg.rows + j * BIG
    for h in range(PARTS):
        for r in range(cfg.groups):
            base = (jnp.bitwise_xor(z, r) * cfg.local + h * cfg.ne) * cfg.cap
            outs[h * cfg.groups + r][...] = dot(onehot(keys - base == target), stacked).astype(BF16)


def hidden_kernel(cfg, h, pos_ref, *refs):
    srcs = refs[: cfg.sources]
    gate_hbm, up_hbm, out_ref, gate, up, rows, sems = refs[cfg.sources:]
    kb = cfg.kb
    depth = gate.shape[1] // kb
    copies = []
    for e in range(cfg.ne):
        for k in range(kb):
            part = pl.ds(k * depth, depth)
            pair = []
            for m, (src, dst) in enumerate(((gate_hbm, gate), (up_hbm, up))):
                cp = pltpu.make_async_copy(src.at[h * cfg.ne + e, part], dst.at[e, part], sems.at[(e * kb + k) * 2 + m])
                cp.start()
                pair.append(cp)
            copies.append(pair)
    je = cfg.nd * cfg.ne
    i, c = iota((je * 16, 1), 0), iota((1, 2 * cfg.rp), 1)
    slot = i & 7
    want = ((i >> 3) & 1) * cfg.rp + (i >> 4) * cfg.cap + slot
    spread = onehot((want == c) & (slot < cfg.cap))
    for k in range(cfg.sources // 2):
        pair = jnp.concatenate([srcs[2 * k][...], srcs[2 * k + 1][...]], axis=0)
        spaced = dot(spread, pair).astype(BF16)
        for j in range(cfg.nd):
            for e in range(cfg.ne):
                at = (j * cfg.ne + e) * 16
                rows[e, k * 16:(k + 1) * 16, j * cfg.w:(j + 1) * cfg.w] = spaced[at:at + 16]
    per = cfg.sources * cfg.cap
    i = iota((per, 1), 0)
    s = div(i, cfg.cap)
    slot = i - s * cfg.cap
    rel = jnp.bitwise_xor(s, pos_ref[1] * 2 + pos_ref[2])
    compact = onehot(iota((1, cfg.sources * 8), 1) == rel * 8 + slot)
    for e in range(cfg.ne):
        g = u = 0.0
        for k in range(kb):
            for cp in copies[e * kb + k]:
                cp.wait()
            x = rows[e, :, k * depth:(k + 1) * depth]
            g = g + dot(x, gate[e, k * depth:(k + 1) * depth])
            u = u + dot(x, up[e, k * depth:(k + 1) * depth])
        hid = (g / (1.0 + jnp.exp(-g)) * u).astype(BF16)
        out_ref[e * per:(e + 1) * per] = dot(compact, hid).astype(BF16)


def down_kernel(cfg, h, pos_ref, own, x, core, xcore, down_hbm, *refs):
    outs = refs[: cfg.groups * 2]
    down, full, sems = refs[cfg.groups * 2:]
    c, t = pos_ref[1], pos_ref[2]
    copies = []
    for e in range(cfg.ne):
        cp = pltpu.make_async_copy(down_hbm.at[h * cfg.ne + e], down.at[e], sems.at[e])
        cp.start()
        copies.append(cp)
    f = own.shape[1]
    for ref, dc, dt in ((own, 0, 0), (x, 1, 0), (core, 0, 1), (xcore, 1, 1)):
        at = (jnp.bitwise_xor(c, dc) * 2 + jnp.bitwise_xor(t, dt)) * f
        full[:, pl.ds(pl.multiple_of(at, 128), f)] = ref[...]
    per = cfg.sources * cfg.cap
    results = []
    for e in range(cfg.ne):
        copies[e].wait()
        results.append(dot(full[e * per:(e + 1) * per], down[e]).astype(BF16))
    width = down.shape[2] // 2
    stacked = jnp.concatenate([v[:, q * width:(q + 1) * width] for q in range(2) for v in results], axis=0)
    m = iota((4 * cfg.rows, 1), 0)
    qt = div(m, cfg.rows)
    p = m - qt * cfg.rows
    e = div(p, cfg.cap)
    slot = p - e * cfg.cap
    want = (qt >> 1) * (cfg.ne * per) + e * per + (qt & 1) * cfg.cap + slot
    lane = iota((1, 2 * cfg.ne * per), 1)
    for r in range(cfg.groups):
        for dc in range(2):
            place = (r * 2 + jnp.bitwise_xor(c, dc)) * 2 * cfg.cap
            outs[r * 2 + dc][...] = dot(onehot(lane - place == want), stacked).astype(BF16)


def combine_kernel(cfg, pos_ref, ids_own, ids_peer, route_own, route_peer, *refs):
    count = PARTS * cfg.groups * 2
    msgs = refs[:count]
    mine, other = refs[count:]
    z, c, t = pos_ref[0], pos_ref[1], pos_ref[2]
    block = 4 * cfg.rows
    lanes = iota((1, PARTS * cfg.groups * block), 1)
    hr = div(lanes, block)
    m = lanes - hr * block
    hh = div(hr, cfg.groups)
    r = hr - hh * cfg.groups
    qt = div(m, cfg.rows)
    p = m - qt * cfg.rows
    code = (jnp.bitwise_xor(r, z) * cfg.local + hh * cfg.ne) * cfg.cap + p + qt * BIG
    picks = []
    for rel, ids in enumerate((ids_own, ids_peer)):
        key = as_column(slot_keys(ids[...], cfg.cap))
        for q in range(2):
            picks.append(onehot(key + (q * 2 + jnp.bitwise_xor(t, rel)) * BIG == code))
    picks = jnp.concatenate(picks, axis=0)
    n = ids_own.shape[1]
    weights = [as_column(route_own[...]), as_column(route_peer[...])]
    for dc in range(2):
        stacked = jnp.concatenate([msgs[k * 2 + dc][...] for k in range(PARTS * cfg.groups)], axis=0)
        got = dot(picks, stacked)
        width = got.shape[1]
        at = jnp.bitwise_xor(c, dc) * (2 * width)
        for rel, out in enumerate((mine, other)):
            for q in range(2):
                k = rel * 2 + q
                out[:, pl.ds(pl.multiple_of(at + q * width, 128), width)] = (weights[rel] * got[k * n:(k + 1) * n]).astype(BF16)


def join_kernel(pos_ref, mine, other, out):
    t = pos_ref[2]
    width = mine.shape[1] // 2
    for cc in range(2):
        for ref, dt in ((mine, 0), (other, 1)):
            at = cc * 2 * width + jnp.bitwise_xor(t, dt) * width
            out[:, pl.ds(pl.multiple_of(at, 128), width)] = ref[:, cc * width:(cc + 1) * width]


class Sizes:
    pass


def swap(x, axis):
    return lax.ppermute(x, axis, [(0, 1), (1, 0)])


def on_device(tokens, expert_ids, route_weights, gate_weight, up_weight, down_weight):
    cfg = Sizes()
    n, width = tokens.shape
    cfg.groups = lax.axis_size("expert")
    cfg.local = gate_weight.shape[0]
    experts = cfg.groups * cfg.local
    cfg.cap = max(2, n * 5 // (4 * experts))
    cfg.ne = cfg.local // PARTS
    cfg.rows = cfg.ne * cfg.cap
    cfg.nd = 16 // cfg.ne
    cfg.w = width // cfg.nd
    cfg.rp = cfg.rows * cfg.nd
    cfg.sources = cfg.groups * 4
    cfg.kb = 4
    f = gate_weight.shape[2]
    ff, wide = down_weight.shape[1:]
    per = cfg.sources * cfg.cap

    z, c, t = (lax.axis_index(a) for a in ("expert", "context", "tensor"))
    pos = jnp.stack([z, c, t]).astype(I32)
    ids = expert_ids.reshape(1, n)
    route = route_weights.reshape(1, n)
    smem = pl.BlockSpec(memory_space=pltpu.SMEM)
    vmem = pl.BlockSpec(memory_space=pltpu.VMEM)
    hbm = pl.BlockSpec(memory_space=pl.ANY)
    params = pltpu.CompilerParams(vmem_limit_bytes=VMEM_LIMIT)

    def call(kernel, ins, outs, scratch=(), name=None):
        return pl.pallas_call(kernel, in_specs=ins, out_specs=[vmem] * len(outs), out_shape=outs,
                              scratch_shapes=scratch, compiler_params=params, name=name)

    shape = jax.ShapeDtypeStruct
    blocks = call(functools.partial(dispatch_kernel, cfg), [smem, vmem, vmem],
                  [shape((cfg.rp, cfg.w), BF16)] * (PARTS * cfg.groups), name="dispatch")(pos, ids, tokens)
    ids_peer, route_peer = swap(ids, "tensor"), swap(route, "tensor")

    arrived = [[blocks[h * cfg.groups]] + [
        lax.ppermute(blocks[h * cfg.groups + r], "expert", [(i, i ^ r) for i in range(cfg.groups)])
        for r in range(1, cfg.groups)] for h in range(PARTS)]
    returned = []
    for h in range(PARTS):
        sources = []
        for a in arrived[h]:
            ax = swap(a, "context")
            sources += [a, swap(a, "tensor"), ax, swap(ax, "tensor")]
        hid = call(
            functools.partial(hidden_kernel, cfg, h), [smem] + [vmem] * cfg.sources + [hbm, hbm],
            [shape((cfg.ne * per, f), BF16)],
            [pltpu.VMEM((cfg.ne, width, f), BF16), pltpu.VMEM((cfg.ne, width, f), BF16),
             pltpu.VMEM((cfg.ne, cfg.sources * 8, width), BF16),
             pltpu.SemaphoreType.DMA((cfg.ne * cfg.kb * 2,))], name="hidden",
        )(pos, *sources, gate_weight, up_weight)[0]
        hx = swap(hid, "context")
        outs = call(
            functools.partial(down_kernel, cfg, h), [smem] + [vmem] * 4 + [hbm],
            [shape((4 * cfg.rows, wide // 2), BF16)] * (cfg.groups * 2),
            [pltpu.VMEM((cfg.ne, ff, wide), BF16), pltpu.VMEM((cfg.ne * per, ff), BF16),
             pltpu.SemaphoreType.DMA((cfg.ne,))], name="down",
        )(pos, hid, hx, swap(hid, "tensor"), swap(hx, "tensor"), down_weight)
        for r in range(cfg.groups):
            for dc in range(2):
                o = outs[r * 2 + dc]
                if r or dc:
                    o = lax.ppermute(o, ("expert", "context"), [
                        (i * 2 + k, (i ^ r) * 2 + (k ^ dc)) for i in range(cfg.groups) for k in range(2)])
                returned.append(o)
    mine, other = call(
        functools.partial(combine_kernel, cfg), [smem] + [vmem] * (4 + len(returned)),
        [shape((n, 2 * wide), BF16)] * 2, name="combine")(pos, ids, ids_peer, route, route_peer, *returned)
    return call(join_kernel, [smem, vmem, vmem], [shape((n, width), BF16)], name="join")(
        pos, mine, swap(other, "tensor"))[0]


def by_gathers(tokens, expert_ids, route_weights, gate_weight, up_weight, down_weight):
    n, width = tokens.shape
    local = gate_weight.shape[0]
    groups = lax.axis_size("expert")
    experts = local * groups
    cap = max(2, n * 5 // (4 * experts))
    ids = expert_ids[:, 0]
    member = (ids[:, None] == jnp.arange(experts, dtype=I32)[None, :]).astype(I32)
    rank = jnp.sum((jnp.cumsum(member, axis=0) - 1) * member, axis=1)
    key = ids * cap + rank
    pick = onehot(key[:, None] == jnp.arange(experts * cap, dtype=I32)[None, :])
    out = jnp.dot(pick.T, tokens, preferred_element_type=F32).astype(BF16)
    out = out.reshape(groups, local, cap, width).transpose(1, 0, 2, 3)
    inc = lax.all_to_all(out, "expert", split_axis=1, concat_axis=1, tiled=True)
    inc = inc.reshape(local, groups * cap, width)
    rows = lax.all_gather(inc, ("context", "tensor"), axis=1, tiled=True)
    g = jnp.einsum("end,edf->enf", rows, gate_weight, preferred_element_type=F32)
    u = jnp.einsum("end,edf->enf", rows, up_weight, preferred_element_type=F32)
    hid = (jax.nn.silu(g) * u).astype(BF16)
    hid = lax.all_gather(hid, ("context", "tensor"), axis=2, tiled=True)
    res = jnp.einsum("erf,efd->erd", hid, down_weight, preferred_element_type=F32).astype(BF16)
    back = lax.all_to_all(res, ("context", "tensor"), split_axis=1, concat_axis=2, tiled=True)
    back = back.reshape(local, groups, cap, width)
    back = lax.all_to_all(back, "expert", split_axis=1, concat_axis=1, tiled=True)
    back = back.transpose(1, 0, 2, 3).reshape(experts * cap, width)
    picked = jnp.dot(pick, back, preferred_element_type=F32)
    return (route_weights * picked).astype(BF16)


def solution(mesh):
    size = dict(mesh.shape)
    paired = size["context"] == 2 and size["tensor"] == 2 and size["expert"] == 4
    rows = P(("group", "expert", "context", "tensor"), None)
    weights = P("expert", None, ("context", "tensor"))
    return jax.shard_map(
        on_device if paired else by_gathers,
        mesh=mesh,
        in_specs=(rows, rows, rows, weights, weights, weights),
        out_specs=rows,
        check_vma=False,
    )
```

```python
import functools
import jax
import jax.numpy as jnp
from jax import lax
from jax.experimental import pallas as pl
from jax.experimental.pallas import tpu as pltpu
from jax.sharding import PartitionSpec as P

BIG = 4096
PARTS = 1
LEAD = 20 * 10**9
VMEM_LIMIT = 16 * 1024 * 1024
F32, BF16, I32 = jnp.float32, jnp.bfloat16, jnp.int32


def div(x, by):
    return ((x.astype(F32) + 0.5) * (1.0 / by)).astype(I32)


def onehot(cond):
    return jnp.where(cond, 1.0, 0.0).astype(BF16)


def dot(a, b):
    return jnp.dot(a, b, preferred_element_type=F32)


def iota(shape, dim):
    return lax.broadcasted_iota(I32, shape, dim)


def as_column(row):
    n = row.shape[1]
    square = jnp.broadcast_to(row, (n, n))
    return jnp.sum(jnp.where(iota((n, n), 0) == iota((n, n), 1), square, jnp.zeros((), row.dtype)), axis=1, keepdims=True)


def slot_keys(ids_row, cap):
    n = ids_row.shape[1]
    ids_col = as_column(ids_row)
    earlier = (ids_col == ids_row) & (iota((n, n), 0) < iota((n, n), 1))
    rank = jnp.sum(jnp.where(earlier, 1, 0), axis=0, keepdims=True)
    return ids_row * cap + rank


def dispatch_kernel(cfg, pos_ref, ids_ref, tok_ref, *outs):
    z = pos_ref[0]
    n = tok_ref.shape[0]
    keys = slot_keys(ids_ref[...], cfg.cap)
    keys = jnp.concatenate([keys + j * BIG for j in range(cfg.nd)], axis=1)
    stacked = jnp.concatenate([tok_ref[:, j * cfg.w:(j + 1) * cfg.w] for j in range(cfg.nd)], axis=0)
    i = iota((cfg.rp, 1), 0)
    j = div(i, cfg.rows)
    target = i - j * cfg.rows + j * BIG
    for h in range(PARTS):
        for r in range(cfg.groups):
            base = (jnp.bitwise_xor(z, r) * cfg.local + h * cfg.ne) * cfg.cap
            outs[h * cfg.groups + r][...] = dot(onehot(keys - base == target), stacked).astype(BF16)


def hidden_kernel(cfg, h, pos_ref, *refs):
    srcs = refs[: cfg.sources]
    gate, up, out_ref, rows = refs[cfg.sources:]
    je = cfg.nd * cfg.ne
    i, c = iota((je * 16, 1), 0), iota((1, 2 * cfg.rp), 1)
    slot = i & 7
    want = ((i >> 3) & 1) * cfg.rp + (i >> 4) * cfg.cap + slot
    spread = onehot((want == c) & (slot < cfg.cap))
    for k in range(cfg.sources // 2):
        pair = jnp.concatenate([srcs[2 * k][...], srcs[2 * k + 1][...]], axis=0)
        spaced = dot(spread, pair).astype(BF16)
        for j in range(cfg.nd):
            for e in range(cfg.ne):
                at = (j * cfg.ne + e) * 16
                rows[e, k * 16:(k + 1) * 16, j * cfg.w:(j + 1) * cfg.w] = spaced[at:at + 16]
    per = cfg.sources * cfg.cap
    i = iota((per, 1), 0)
    s = div(i, cfg.cap)
    slot = i - s * cfg.cap
    rel = jnp.bitwise_xor(s, pos_ref[1] * 2 + pos_ref[2])
    compact = onehot(iota((1, cfg.sources * 8), 1) == rel * 8 + slot)
    for e in range(cfg.ne):
        both = dot(rows[e], jnp.concatenate([gate[h * cfg.ne + e], up[h * cfg.ne + e]], axis=1))
        g, u = jnp.split(both, 2, axis=1)
        hid = (g / (1.0 + jnp.exp(-g)) * u).astype(BF16)
        out_ref[e * per:(e + 1) * per] = dot(compact, hid).astype(BF16)


def down_kernel(cfg, h, pos_ref, own, x, core, xcore, down, *refs):
    outs = refs[: cfg.groups * 2]
    full = refs[cfg.groups * 2]
    c, t = pos_ref[1], pos_ref[2]
    f = own.shape[1]
    for ref, dc, dt in ((own, 0, 0), (x, 1, 0), (core, 0, 1), (xcore, 1, 1)):
        at = (jnp.bitwise_xor(c, dc) * 2 + jnp.bitwise_xor(t, dt)) * f
        full[:, pl.ds(pl.multiple_of(at, 128), f)] = ref[...]
    per = cfg.sources * cfg.cap
    results = []
    for e in range(cfg.ne):
        results.append(dot(full[e * per:(e + 1) * per], down[h * cfg.ne + e]).astype(BF16))
    width = down.shape[2] // 2
    stacked = jnp.concatenate([v[:, q * width:(q + 1) * width] for q in range(2) for v in results], axis=0)
    m = iota((4 * cfg.rows, 1), 0)
    qt = div(m, cfg.rows)
    p = m - qt * cfg.rows
    e = div(p, cfg.cap)
    slot = p - e * cfg.cap
    want = (qt >> 1) * (cfg.ne * per) + e * per + (qt & 1) * cfg.cap + slot
    lane = iota((1, 2 * cfg.ne * per), 1)
    for r in range(cfg.groups):
        for dc in range(2):
            place = (r * 2 + jnp.bitwise_xor(c, dc)) * 2 * cfg.cap
            outs[r * 2 + dc][...] = dot(onehot(lane - place == want), stacked).astype(BF16)


def combine_kernel(cfg, pos_ref, ids_own, ids_peer, route_own, route_peer, *refs):
    count = PARTS * cfg.groups * 2
    msgs = refs[:count]
    mine, other = refs[count:]
    z, c, t = pos_ref[0], pos_ref[1], pos_ref[2]
    block = 4 * cfg.rows
    lanes = iota((1, PARTS * cfg.groups * block), 1)
    hr = div(lanes, block)
    m = lanes - hr * block
    hh = div(hr, cfg.groups)
    r = hr - hh * cfg.groups
    qt = div(m, cfg.rows)
    p = m - qt * cfg.rows
    code = (jnp.bitwise_xor(r, z) * cfg.local + hh * cfg.ne) * cfg.cap + p + qt * BIG
    picks = []
    for rel, ids in enumerate((ids_own, ids_peer)):
        key = as_column(slot_keys(ids[...], cfg.cap))
        for q in range(2):
            picks.append(onehot(key + (q * 2 + jnp.bitwise_xor(t, rel)) * BIG == code))
    picks = jnp.concatenate(picks, axis=0)
    n = ids_own.shape[1]
    weights = [as_column(route_own[...]), as_column(route_peer[...])]
    for dc in range(2):
        stacked = jnp.concatenate([msgs[k * 2 + dc][...] for k in range(PARTS * cfg.groups)], axis=0)
        got = dot(picks, stacked)
        width = got.shape[1]
        at = jnp.bitwise_xor(c, dc) * (2 * width)
        for rel, out in enumerate((mine, other)):
            for q in range(2):
                k = rel * 2 + q
                out[:, pl.ds(pl.multiple_of(at + q * width, 128), width)] = (weights[rel] * got[k * n:(k + 1) * n]).astype(BF16)


def join_kernel(pos_ref, mine, other, out):
    t = pos_ref[2]
    width = mine.shape[1] // 2
    for cc in range(2):
        for ref, dt in ((mine, 0), (other, 1)):
            at = cc * 2 * width + jnp.bitwise_xor(t, dt) * width
            out[:, pl.ds(pl.multiple_of(at, 128), width)] = ref[:, cc * width:(cc + 1) * width]


class Sizes:
    pass


def swap(x, axis):
    return lax.ppermute(x, axis, [(0, 1), (1, 0)])


def on_device(tokens, expert_ids, route_weights, gate_weight, up_weight, down_weight):
    cfg = Sizes()
    n, width = tokens.shape
    cfg.groups = lax.axis_size("expert")
    cfg.local = gate_weight.shape[0]
    experts = cfg.groups * cfg.local
    cfg.cap = max(2, n * 5 // (4 * experts))
    cfg.ne = cfg.local // PARTS
    cfg.rows = cfg.ne * cfg.cap
    cfg.nd = 16 // cfg.ne
    cfg.w = width // cfg.nd
    cfg.rp = cfg.rows * cfg.nd
    cfg.sources = cfg.groups * 4
    f = gate_weight.shape[2]
    ff, wide = down_weight.shape[1:]
    per = cfg.sources * cfg.cap

    z, c, t = (lax.axis_index(a) for a in ("expert", "context", "tensor"))
    pos = jnp.stack([z, c, t]).astype(I32)
    ids = expert_ids.reshape(1, n)
    route = route_weights.reshape(1, n)
    smem = pl.BlockSpec(memory_space=pltpu.SMEM)
    vmem = pl.BlockSpec(memory_space=pltpu.VMEM)
    params = pltpu.CompilerParams(vmem_limit_bytes=VMEM_LIMIT)

    def call(kernel, ins, outs, scratch=(), name=None, cost=None):
        return pl.pallas_call(kernel, in_specs=ins, out_specs=[vmem] * len(outs), out_shape=outs,
                              scratch_shapes=scratch, compiler_params=params, name=name, cost_estimate=cost)

    shape = jax.ShapeDtypeStruct
    blocks = call(functools.partial(dispatch_kernel, cfg), [smem, vmem, vmem],
                  [shape((cfg.rp, cfg.w), BF16)] * (PARTS * cfg.groups), name="dispatch",
                  cost=pl.CostEstimate(flops=LEAD, bytes_accessed=0, transcendentals=0))(pos, ids, tokens)
    ids_peer, route_peer = swap(ids, "tensor"), swap(route, "tensor")

    arrived = [[blocks[h * cfg.groups]] + [
        lax.ppermute(blocks[h * cfg.groups + r], "expert", [(i, i ^ r) for i in range(cfg.groups)])
        for r in range(1, cfg.groups)] for h in range(PARTS)]
    returned = []
    for h in range(PARTS):
        near = [swap(a, "context") for a in arrived[h][:2]]
        far = arrived[h][2:]
        far2 = []
        for a in far:
            a, n1 = lax.optimization_barrier((a, near[1]))
            far2.append(a)
            near[1] = n1
        far = far2
        sources = []
        for a, ax in zip(arrived[h][:2] + far, near + [swap(a, "context") for a in far]):
            sources += [a, swap(a, "tensor"), ax, swap(ax, "tensor")]
        hid = call(
            functools.partial(hidden_kernel, cfg, h), [smem] + [vmem] * (cfg.sources + 2),
            [shape((cfg.ne * per, f), BF16)],
            [pltpu.VMEM((cfg.ne, cfg.sources * 8, width), BF16)], name="hidden",
        )(pos, *sources, gate_weight, up_weight)[0]
        hx = swap(hid, "context")
        outs = call(
            functools.partial(down_kernel, cfg, h), [smem] + [vmem] * 5,
            [shape((4 * cfg.rows, wide // 2), BF16)] * (cfg.groups * 2),
            [pltpu.VMEM((cfg.ne * per, ff), BF16)], name="down",
        )(pos, hid, hx, swap(hid, "tensor"), swap(hx, "tensor"), down_weight)
        for r in range(cfg.groups):
            for dc in range(2):
                o = outs[r * 2 + dc]
                if r or dc:
                    o = lax.ppermute(o, ("expert", "context"), [
                        (i * 2 + k, (i ^ r) * 2 + (k ^ dc)) for i in range(cfg.groups) for k in range(2)])
                returned.append(o)
    mine, other = call(
        functools.partial(combine_kernel, cfg), [smem] + [vmem] * (4 + len(returned)),
        [shape((n, 2 * wide), BF16)] * 2, name="combine")(pos, ids, ids_peer, route, route_peer, *returned)
    return call(join_kernel, [smem, vmem, vmem], [shape((n, width), BF16)], name="join")(
        pos, mine, swap(other, "tensor"))[0]


def by_gathers(tokens, expert_ids, route_weights, gate_weight, up_weight, down_weight):
    n, width = tokens.shape
    local = gate_weight.shape[0]
    groups = lax.axis_size("expert")
    experts = local * groups
    cap = max(2, n * 5 // (4 * experts))
    ids = expert_ids[:, 0]
    member = (ids[:, None] == jnp.arange(experts, dtype=I32)[None, :]).astype(I32)
    rank = jnp.sum((jnp.cumsum(member, axis=0) - 1) * member, axis=1)
    key = ids * cap + rank
    pick = onehot(key[:, None] == jnp.arange(experts * cap, dtype=I32)[None, :])
    out = jnp.dot(pick.T, tokens, preferred_element_type=F32).astype(BF16)
    out = out.reshape(groups, local, cap, width).transpose(1, 0, 2, 3)
    inc = lax.all_to_all(out, "expert", split_axis=1, concat_axis=1, tiled=True)
    inc = inc.reshape(local, groups * cap, width)
    rows = lax.all_gather(inc, ("context", "tensor"), axis=1, tiled=True)
    g = jnp.einsum("end,edf->enf", rows, gate_weight, preferred_element_type=F32)
    u = jnp.einsum("end,edf->enf", rows, up_weight, preferred_element_type=F32)
    hid = (jax.nn.silu(g) * u).astype(BF16)
    hid = lax.all_gather(hid, ("context", "tensor"), axis=2, tiled=True)
    res = jnp.einsum("erf,efd->erd", hid, down_weight, preferred_element_type=F32).astype(BF16)
    back = lax.all_to_all(res, ("context", "tensor"), split_axis=1, concat_axis=2, tiled=True)
    back = back.reshape(local, groups, cap, width)
    back = lax.all_to_all(back, "expert", split_axis=1, concat_axis=1, tiled=True)
    back = back.transpose(1, 0, 2, 3).reshape(experts * cap, width)
    picked = jnp.dot(pick, back, preferred_element_type=F32)
    return (route_weights * picked).astype(BF16)


def solution(mesh):
    size = dict(mesh.shape)
    paired = size["context"] == 2 and size["tensor"] == 2 and size["expert"] == 4
    rows = P(("group", "expert", "context", "tensor"), None)
    weights = P("expert", None, ("context", "tensor"))
    return jax.shard_map(
        on_device if paired else by_gathers,
        mesh=mesh,
        in_specs=(rows, rows, rows, weights, weights, weights),
        out_specs=rows,
        check_vma=False,
    )
```

```python
import functools
import jax
import jax.numpy as jnp
from jax import lax
from jax.experimental import pallas as pl
from jax.experimental.pallas import tpu as pltpu
from jax.sharding import PartitionSpec as P

BIG = 4096
ORDER = (0, 3, 2, 1, 5, 4, 7, 6)
LEAD = 20 * 10**9
STEP = 10 * 10**9
VMEM_LIMIT = 8 * 1024 * 1024
F32, BF16, I32 = jnp.float32, jnp.bfloat16, jnp.int32


def div(x, by):
    return ((x.astype(F32) + 0.5) * (1.0 / by)).astype(I32)


def onehot(cond):
    return jnp.where(cond, 1.0, 0.0).astype(BF16)


def dot(a, b):
    return jnp.dot(a, b, preferred_element_type=F32)


def iota(shape, dim):
    return lax.broadcasted_iota(I32, shape, dim)


def as_column(row):
    n = row.shape[1]
    square = jnp.broadcast_to(row, (n, n))
    return jnp.sum(jnp.where(iota((n, n), 0) == iota((n, n), 1), square, jnp.zeros((), row.dtype)), axis=1, keepdims=True)


def slot_keys(ids_row, cap):
    n = ids_row.shape[1]
    ids_col = as_column(ids_row)
    earlier = (ids_col == ids_row) & (iota((n, n), 0) < iota((n, n), 1))
    rank = jnp.sum(jnp.where(earlier, 1, 0), axis=0, keepdims=True)
    return ids_row * cap + rank


def dispatch_kernel(cfg, pos_ref, ids_ref, route_ref, tok_ref, *outs):
    z = pos_ref[0]
    keys = slot_keys(ids_ref[...], cfg.cap)
    outs[-1][0:1] = keys.astype(F32)
    outs[-1][1:2] = route_ref[...]
    keys = jnp.concatenate([keys + j * BIG for j in range(cfg.nd)], axis=1)
    stacked = jnp.concatenate([tok_ref[:, j * cfg.w:(j + 1) * cfg.w] for j in range(cfg.nd)], axis=0)
    i = iota((cfg.rp, 1), 0)
    j = div(i, cfg.rows)
    target = i - j * cfg.rows + j * BIG
    for r in range(cfg.groups):
        base = jnp.bitwise_xor(z, r) * cfg.local * cfg.cap
        outs[r][...] = dot(onehot(keys - base == target), stacked).astype(BF16)


def place(cfg, srcs, store):
    i, c = iota((cfg.nd * cfg.ne * 16, 1), 0), iota((1, 2 * cfg.rp), 1)
    slot = i & 7
    want = ((i >> 3) & 1) * cfg.rp + (i >> 4) * cfg.cap + slot
    spread = onehot((want == c) & (slot < cfg.cap))
    for k in range(len(srcs) // 2):
        pair = jnp.concatenate([srcs[2 * k][...], srcs[2 * k + 1][...]], axis=0)
        spaced = dot(spread, pair).astype(BF16)
        for j in range(cfg.nd):
            for e in range(cfg.ne):
                at = (j * cfg.ne + e) * 16
                store(e, k, j, spaced[at:at + 16])


def near_kernel(cfg, pos_ref, *refs):
    rows = refs[-1]

    def store(e, k, j, v):
        rows[e, k * 16:(k + 1) * 16, j * cfg.w:(j + 1) * cfg.w] = v

    place(cfg, refs[:cfg.early * 4], store)


def hidden_rows(cfg, pos_ref, near, far, gate, up, out_ref, first):
    per = cfg.sources * cfg.cap
    i = iota((per, 1), 0)
    s = div(i, cfg.cap)
    slot = i - s * cfg.cap
    rel = jnp.bitwise_xor(s, pos_ref[1] * 2 + pos_ref[2])
    compact = onehot(iota((1, cfg.sources * 8), 1) == rel * 8 + slot)
    for k in range(cfg.ne // 2):
        e = first + k
        x = jnp.concatenate([near[e], far[k]], axis=0)
        both = dot(x, jnp.concatenate([gate[e], up[e]], axis=1))
        g, u = jnp.split(both, 2, axis=1)
        hid = (g / (1.0 + jnp.exp(-g)) * u).astype(BF16)
        out_ref[k * per:(k + 1) * per] = dot(compact, hid).astype(BF16)


def hidden_first_kernel(cfg, pos_ref, *refs):
    late = cfg.sources - cfg.early * 4
    near, gate, up, out_ref, later, now = refs[late:]

    def store(e, k, j, v):
        ref = now if e < cfg.ne // 2 else later
        ref[e % (cfg.ne // 2), k * 16:(k + 1) * 16, j * cfg.w:(j + 1) * cfg.w] = v

    place(cfg, refs[:late], store)
    hidden_rows(cfg, pos_ref, near, now, gate, up, out_ref, 0)


def hidden_second_kernel(cfg, pos_ref, near, far, gate, up, out_ref):
    hidden_rows(cfg, pos_ref, near, far, gate, up, out_ref, cfg.ne // 2)


def down_rows(cfg, pos_ref, parts, down, full, out, first):
    c, t = pos_ref[1], pos_ref[2]
    f = parts[0].shape[1]
    for ref, dc, dt in zip(parts, (0, 1, 0, 1), (0, 0, 1, 1)):
        at = (jnp.bitwise_xor(c, dc) * 2 + jnp.bitwise_xor(t, dt)) * f
        full[:, pl.ds(pl.multiple_of(at, 128), f)] = ref[...]
    per = cfg.sources * cfg.cap
    for k in range(cfg.ne // 2):
        out[k * per:(k + 1) * per] = dot(full[k * per:(k + 1) * per], down[first + k]).astype(BF16)


def sort_rows(cfg, pos_ref, halves, outs):
    per = cfg.sources * cfg.cap
    width = halves[0].shape[1] // 2
    stacked = jnp.concatenate([v[:, q * width:(q + 1) * width] for q in range(2) for v in halves], axis=0)
    m = iota((4 * cfg.rows, 1), 0)
    qt = div(m, cfg.rows)
    p = m - qt * cfg.rows
    e = div(p, cfg.cap)
    slot = p - e * cfg.cap
    want = (qt >> 1) * (cfg.ne * per) + e * per + (qt & 1) * cfg.cap + slot
    lane = iota((1, 2 * cfg.ne * per), 1)
    for k, out in enumerate(outs):
        r, dc = divmod(k, 2)
        place_at = (r * 2 + jnp.bitwise_xor(pos_ref[1], dc)) * 2 * cfg.cap
        out[...] = dot(onehot(lane - place_at == want), stacked).astype(BF16)


def down_first_kernel(cfg, pos_ref, own, x, core, xcore, down, out, full):
    down_rows(cfg, pos_ref, (own, x, core, xcore), down, full, out, 0)


def down_second_kernel(cfg, pos_ref, own, x, core, xcore, down, before, *refs):
    outs, full, out = refs[:-2], refs[-2], refs[-1]
    down_rows(cfg, pos_ref, (own, x, core, xcore), down, full, out, cfg.ne // 2)
    sort_rows(cfg, pos_ref, (before, out), outs)


def combine_kernel(cfg, pos_ref, info_own, info_peer, *refs):
    msgs, (mine, other) = refs[:-2], refs[-2:]
    z, c, t = pos_ref[0], pos_ref[1], pos_ref[2]
    block = 4 * cfg.rows
    lanes = iota((1, cfg.groups * block), 1)
    r = div(lanes, block)
    m = lanes - r * block
    qt = div(m, cfg.rows)
    code = jnp.bitwise_xor(r, z) * cfg.local * cfg.cap + m - qt * cfg.rows + qt * BIG
    picks, weights = [], []
    for rel, info in enumerate((info_own, info_peer)):
        key = as_column(info[0:1]).astype(I32)
        weights.append(as_column(info[1:2]))
        picks += [onehot(key + (q * 2 + jnp.bitwise_xor(t, rel)) * BIG == code) for q in range(2)]
    picks = jnp.concatenate(picks, axis=0)
    n = info_own.shape[1]
    for dc in range(2):
        stacked = jnp.concatenate([msgs[k * 2 + dc][...] for k in range(cfg.groups)], axis=0)
        got = dot(picks, stacked)
        width = got.shape[1]
        at = jnp.bitwise_xor(c, dc) * (2 * width)
        for rel, out in enumerate((mine, other)):
            for q in range(2):
                k = rel * 2 + q
                out[:, pl.ds(pl.multiple_of(at + q * width, 128), width)] = (weights[rel] * got[k * n:(k + 1) * n]).astype(BF16)


def join_kernel(cfg, pos_ref, mine, other, out):
    t = pos_ref[2]
    width = mine.shape[1] // 2
    for cc in range(2):
        for ref, dt in ((mine, 0), (other, 1)):
            at = cc * 2 * width + jnp.bitwise_xor(t, dt) * width
            out[:, pl.ds(pl.multiple_of(at, 128), width)] = ref[:, cc * width:(cc + 1) * width]


class Sizes:
    pass


def swap(x, axis):
    return lax.ppermute(x, axis, [(0, 1), (1, 0)])


def on_device(tokens, expert_ids, route_weights, gate_weight, up_weight, down_weight):
    cfg = Sizes()
    n, width = tokens.shape
    cfg.groups = lax.axis_size("expert")
    cfg.local = gate_weight.shape[0]
    experts = cfg.groups * cfg.local
    cfg.cap = max(2, n * 5 // (4 * experts))
    cfg.ne = cfg.local
    cfg.rows = cfg.ne * cfg.cap
    cfg.nd = 16 // cfg.ne
    cfg.w = width // cfg.nd
    cfg.rp = cfg.rows * cfg.nd
    cfg.sources = cfg.groups * 4
    cfg.early = cfg.groups - 1
    f = gate_weight.shape[2]
    ff, wide = down_weight.shape[1:]
    per = cfg.sources * cfg.cap

    z, c, t = (lax.axis_index(a) for a in ("expert", "context", "tensor"))
    pos = jnp.stack([z, c, t]).astype(I32)
    ids = expert_ids.reshape(1, n)
    route = route_weights.reshape(1, n)
    smem = pl.BlockSpec(memory_space=pltpu.SMEM)
    vmem = pl.BlockSpec(memory_space=pltpu.VMEM)
    params = pltpu.CompilerParams(vmem_limit_bytes=VMEM_LIMIT)
    shape = jax.ShapeDtypeStruct

    def call(kernel, name, ins, outs, scratch=(), work=10**9):
        args = [pos] + list(ins)
        return list(pl.pallas_call(
            kernel, in_specs=[smem] + [vmem] * len(ins), out_specs=[vmem] * len(outs),
            out_shape=[o if isinstance(o, shape) else shape(o, BF16) for o in outs], scratch_shapes=scratch, compiler_params=params, name=name,
            cost_estimate=pl.CostEstimate(flops=work, bytes_accessed=0, transcendentals=0))(*args))

    def kernel(f):
        return functools.partial(f, cfg)

    *blocks, info = call(kernel(dispatch_kernel), "dispatch", [ids, route, tokens],
                         [(cfg.rp, cfg.w)] * cfg.groups + [shape((2, n), F32)], work=LEAD)
    info_peer = swap(info, "tensor")

    def move(x, r, dc):
        return lax.ppermute(x, ("expert", "context"), [
            (i * 2 + k, (i ^ r) * 2 + (k ^ dc)) for i in range(cfg.groups) for k in range(2)])

    half = cfg.ne // 2
    early, late = cfg.early * 32, (cfg.groups - cfg.early) * 32
    far = move(blocks[3], 3, 0)
    mid = move(blocks[2], 2, 0)
    one = move(blocks[1], 1, 0)
    close = [blocks[0], swap(blocks[0], "context"), one, move(blocks[1], 1, 1), mid, swap(mid, "context")]
    near = call(kernel(near_kernel), "near", [b for a in close for b in (a, swap(a, "tensor"))] + [info_peer],
                [(cfg.ne, early, width)])[0]
    crossed = swap(far, "context")
    near, crossed = lax.optimization_barrier((near, crossed))
    far = [far, swap(far, "tensor"), crossed, swap(crossed, "tensor")]
    hid_a, later = call(kernel(hidden_first_kernel), "hidden_a", far + [near, gate_weight, up_weight],
                        [(half * per, f), (half, late, width)], [pltpu.VMEM((half, late, width), BF16)], work=STEP)
    xa = swap(hid_a, "context")
    hid_b = call(kernel(hidden_second_kernel), "hidden_b", [near, later, gate_weight, up_weight],
                 [(half * per, f)], work=STEP)[0]
    xb = swap(hid_b, "context")
    full = pltpu.VMEM((half * per, ff), BF16)
    out_a = call(kernel(down_first_kernel), "down_a", [hid_a, xa, swap(hid_a, "tensor"), swap(xa, "tensor"), down_weight],
                 [(half * per, wide)], [full], work=STEP)[0]
    message = (4 * cfg.rows, wide // 2)
    outs = call(
        kernel(down_second_kernel), "down_b",
        [hid_b, xb, swap(hid_b, "tensor"), swap(xb, "tensor"), down_weight, out_a],
        [message] * (cfg.groups * 2), [full, pltpu.VMEM((half * per, wide), BF16)], work=STEP)
    returned = [outs[0]] + [move(o, k // 2, k % 2) for k, o in enumerate(outs) if k]
    order = ORDER
    mine, other = call(
        lambda pos_ref, own, peer, *refs: combine_kernel(
            cfg, pos_ref, own, peer, *[refs[order.index(k)] for k in range(len(order))], *refs[len(order):]),
        "combine", [info, info_peer] + [returned[k] for k in order], [(n, 2 * wide)] * 2)
    return call(kernel(join_kernel), "join", [mine, swap(other, "tensor")], [(n, width)])[0]


def by_gathers(tokens, expert_ids, route_weights, gate_weight, up_weight, down_weight):
    n, width = tokens.shape
    local = gate_weight.shape[0]
    groups = lax.axis_size("expert")
    experts = local * groups
    cap = max(2, n * 5 // (4 * experts))
    ids = expert_ids[:, 0]
    member = (ids[:, None] == jnp.arange(experts, dtype=I32)[None, :]).astype(I32)
    rank = jnp.sum((jnp.cumsum(member, axis=0) - 1) * member, axis=1)
    key = ids * cap + rank
    pick = onehot(key[:, None] == jnp.arange(experts * cap, dtype=I32)[None, :])
    out = jnp.dot(pick.T, tokens, preferred_element_type=F32).astype(BF16)
    out = out.reshape(groups, local, cap, width).transpose(1, 0, 2, 3)
    inc = lax.all_to_all(out, "expert", split_axis=1, concat_axis=1, tiled=True)
    inc = inc.reshape(local, groups * cap, width)
    rows = lax.all_gather(inc, ("context", "tensor"), axis=1, tiled=True)
    g = jnp.einsum("end,edf->enf", rows, gate_weight, preferred_element_type=F32)
    u = jnp.einsum("end,edf->enf", rows, up_weight, preferred_element_type=F32)
    hid = (jax.nn.silu(g) * u).astype(BF16)
    hid = lax.all_gather(hid, ("context", "tensor"), axis=2, tiled=True)
    res = jnp.einsum("erf,efd->erd", hid, down_weight, preferred_element_type=F32).astype(BF16)
    back = lax.all_to_all(res, ("context", "tensor"), split_axis=1, concat_axis=2, tiled=True)
    back = back.reshape(local, groups, cap, width)
    back = lax.all_to_all(back, "expert", split_axis=1, concat_axis=1, tiled=True)
    back = back.transpose(1, 0, 2, 3).reshape(experts * cap, width)
    picked = jnp.dot(pick, back, preferred_element_type=F32)
    return (route_weights * picked).astype(BF16)


def solution(mesh):
    size = dict(mesh.shape)
    paired = size["context"] == 2 and size["tensor"] == 2 and size["expert"] == 4
    rows = P(("group", "expert", "context", "tensor"), None)
    weights = P("expert", None, ("context", "tensor"))
    return jax.shard_map(
        on_device if paired else by_gathers,
        mesh=mesh,
        in_specs=(rows, rows, rows, weights, weights, weights),
        out_specs=rows,
        check_vma=False,
    )
```

```python
import functools
import jax
import jax.numpy as jnp
from jax import lax
from jax.experimental import pallas as pl
from jax.experimental.pallas import tpu as pltpu
from jax.sharding import PartitionSpec as P

BIG = 4096
ORDER = (0, 7, 5, 3, 1, 6, 4, 2)
LEAD = 20 * 10**9
STEP = 10 * 10**9
VMEM_LIMIT = 8 * 1024 * 1024
F32, BF16, I32 = jnp.float32, jnp.bfloat16, jnp.int32


def div(x, by):
    return ((x.astype(F32) + 0.5) * (1.0 / by)).astype(I32)


def onehot(cond):
    return jnp.where(cond, 1.0, 0.0).astype(BF16)


def dot(a, b):
    return jnp.dot(a, b, preferred_element_type=F32)


def iota(shape, dim):
    return lax.broadcasted_iota(I32, shape, dim)


def as_column(row):
    n = row.shape[1]
    square = jnp.broadcast_to(row, (n, n))
    return jnp.sum(jnp.where(iota((n, n), 0) == iota((n, n), 1), square, jnp.zeros((), row.dtype)), axis=1, keepdims=True)


def slot_keys(ids_row, cap):
    n = ids_row.shape[1]
    ids_col = as_column(ids_row)
    earlier = (ids_col == ids_row) & (iota((n, n), 0) < iota((n, n), 1))
    rank = jnp.sum(jnp.where(earlier, 1, 0), axis=0, keepdims=True)
    return ids_row * cap + rank


def dispatch_kernel(cfg, pos_ref, ids_ref, tok_ref, *outs):
    z = pos_ref[0]
    keys = slot_keys(ids_ref[...], cfg.cap)
    keys = jnp.concatenate([keys + j * BIG for j in range(cfg.nd)], axis=1)
    stacked = jnp.concatenate([tok_ref[:, j * cfg.w:(j + 1) * cfg.w] for j in range(cfg.nd)], axis=0)
    i = iota((cfg.rp, 1), 0)
    j = div(i, cfg.rows)
    target = i - j * cfg.rows + j * BIG
    for r in range(cfg.groups):
        base = jnp.bitwise_xor(z, r) * cfg.local * cfg.cap
        outs[r][...] = dot(onehot(keys - base == target), stacked).astype(BF16)


def place(cfg, srcs, store):
    i, c = iota((cfg.nd * cfg.ne * 16, 1), 0), iota((1, 2 * cfg.rp), 1)
    slot = i & 7
    want = ((i >> 3) & 1) * cfg.rp + (i >> 4) * cfg.cap + slot
    spread = onehot((want == c) & (slot < cfg.cap))
    for k in range(len(srcs) // 2):
        pair = jnp.concatenate([srcs[2 * k][...], srcs[2 * k + 1][...]], axis=0)
        spaced = dot(spread, pair).astype(BF16)
        for j in range(cfg.nd):
            for e in range(cfg.ne):
                at = (j * cfg.ne + e) * 16
                store(e, k, j, spaced[at:at + 16])


def near_kernel(cfg, pos_ref, *refs):
    ids_ref, route_ref, rows, info = refs[-4:]
    info[0:1] = slot_keys(ids_ref[...], cfg.cap).astype(F32)
    info[1:2] = route_ref[...]

    def store(e, k, j, v):
        rows[e, k * 16:(k + 1) * 16, j * cfg.w:(j + 1) * cfg.w] = v

    place(cfg, refs[:cfg.early * 4], store)


def hidden_rows(cfg, pos_ref, near, far, gate, up, out_ref, first):
    per = cfg.sources * cfg.cap
    i = iota((per, 1), 0)
    s = div(i, cfg.cap)
    slot = i - s * cfg.cap
    rel = jnp.bitwise_xor(s & 3, pos_ref[1] * 2 + pos_ref[2])
    for k, r in enumerate(cfg.visits):
        rel = rel + jnp.where((s >> 2) == r, 4 * k, 0)
    compact = onehot(iota((1, cfg.sources * 8), 1) == rel * 8 + slot)
    for k in range(cfg.ne // 2):
        e = first + k
        x = jnp.concatenate([near[e], far[k]], axis=0)
        both = dot(x, jnp.concatenate([gate[e], up[e]], axis=1))
        g, u = jnp.split(both, 2, axis=1)
        hid = (g / (1.0 + jnp.exp(-g)) * u).astype(BF16)
        out_ref[k * per:(k + 1) * per] = dot(compact, hid).astype(BF16)


def hidden_first_kernel(cfg, pos_ref, *refs):
    late = cfg.sources - cfg.early * 4
    near, gate, up, out_ref, later, now = refs[late:]

    def store(e, k, j, v):
        ref = now if e < cfg.ne // 2 else later
        ref[e % (cfg.ne // 2), k * 16:(k + 1) * 16, j * cfg.w:(j + 1) * cfg.w] = v

    place(cfg, refs[:late], store)
    hidden_rows(cfg, pos_ref, near, now, gate, up, out_ref, 0)


def hidden_second_kernel(cfg, pos_ref, near, far, gate, up, out_ref):
    hidden_rows(cfg, pos_ref, near, far, gate, up, out_ref, cfg.ne // 2)


def down_rows(cfg, pos_ref, parts, down, full, out, first):
    c, t = pos_ref[1], pos_ref[2]
    f = parts[0].shape[1]
    for ref, dc, dt in zip(parts, (0, 1, 0, 1), (0, 0, 1, 1)):
        at = (jnp.bitwise_xor(c, dc) * 2 + jnp.bitwise_xor(t, dt)) * f
        full[:, pl.ds(pl.multiple_of(at, 128), f)] = ref[...]
    per = cfg.sources * cfg.cap
    for k in range(cfg.ne // 2):
        out[k * per:(k + 1) * per] = dot(full[k * per:(k + 1) * per], down[first + k]).astype(BF16)


def sort_rows(cfg, pos_ref, halves, outs):
    per = cfg.sources * cfg.cap
    width = halves[0].shape[1] // 2
    stacked = jnp.concatenate([v[:, q * width:(q + 1) * width] for q in range(2) for v in halves], axis=0)
    m = iota((4 * cfg.rows, 1), 0)
    qt = div(m, cfg.rows)
    p = m - qt * cfg.rows
    e = div(p, cfg.cap)
    slot = p - e * cfg.cap
    want = (qt >> 1) * (cfg.ne * per) + e * per + (qt & 1) * cfg.cap + slot
    lane = iota((1, 2 * cfg.ne * per), 1)
    for k, out in enumerate(outs):
        r, dc = divmod(k, 2)
        place_at = (r * 2 + jnp.bitwise_xor(pos_ref[1], dc)) * 2 * cfg.cap
        out[...] = dot(onehot(lane - place_at == want), stacked).astype(BF16)


def down_first_kernel(cfg, pos_ref, own, x, core, xcore, down, info, out, full):
    down_rows(cfg, pos_ref, (own, x, core, xcore), down, full, out, 0)


def down_second_kernel(cfg, pos_ref, own, x, core, xcore, down, before, *refs):
    outs, full, out = refs[:-2], refs[-2], refs[-1]
    down_rows(cfg, pos_ref, (own, x, core, xcore), down, full, out, cfg.ne // 2)
    sort_rows(cfg, pos_ref, (before, out), outs)


def combine_kernel(cfg, pos_ref, info_own, info_peer, *refs):
    msgs, (mine, other) = refs[:-2], refs[-2:]
    z, c, t = pos_ref[0], pos_ref[1], pos_ref[2]
    block = 4 * cfg.rows
    lanes = iota((1, cfg.groups * block), 1)
    r = div(lanes, block)
    m = lanes - r * block
    qt = div(m, cfg.rows)
    code = jnp.bitwise_xor(r, z) * cfg.local * cfg.cap + m - qt * cfg.rows + qt * BIG
    picks, weights = [], []
    for rel, info in enumerate((info_own, info_peer)):
        key = as_column(info[0:1]).astype(I32)
        weights.append(as_column(info[1:2]))
        picks += [onehot(key + (q * 2 + jnp.bitwise_xor(t, rel)) * BIG == code) for q in range(2)]
    picks = jnp.concatenate(picks, axis=0)
    n = info_own.shape[1]
    for dc in range(2):
        stacked = jnp.concatenate([msgs[k * 2 + dc][...] for k in range(cfg.groups)], axis=0)
        got = dot(picks, stacked)
        width = got.shape[1]
        at = jnp.bitwise_xor(c, dc) * (2 * width)
        for rel, out in enumerate((mine, other)):
            for q in range(2):
                k = rel * 2 + q
                out[:, pl.ds(pl.multiple_of(at + q * width, 128), width)] = (weights[rel] * got[k * n:(k + 1) * n]).astype(BF16)


def join_kernel(cfg, pos_ref, mine, other, out):
    t = pos_ref[2]
    width = mine.shape[1] // 2
    for cc in range(2):
        for ref, dt in ((mine, 0), (other, 1)):
            at = cc * 2 * width + jnp.bitwise_xor(t, dt) * width
            out[:, pl.ds(pl.multiple_of(at, 128), width)] = ref[:, cc * width:(cc + 1) * width]


class Sizes:
    pass


def swap(x, axis):
    return lax.ppermute(x, axis, [(0, 1), (1, 0)])


def on_device(tokens, expert_ids, route_weights, gate_weight, up_weight, down_weight):
    cfg = Sizes()
    n, width = tokens.shape
    cfg.groups = lax.axis_size("expert")
    cfg.local = gate_weight.shape[0]
    experts = cfg.groups * cfg.local
    cfg.cap = max(2, n * 5 // (4 * experts))
    cfg.ne = cfg.local
    cfg.rows = cfg.ne * cfg.cap
    cfg.nd = 16 // cfg.ne
    cfg.w = width // cfg.nd
    cfg.rp = cfg.rows * cfg.nd
    cfg.sources = cfg.groups * 4
    cfg.early = 3
    cfg.visits = (0, 1, 2, 3)
    f = gate_weight.shape[2]
    ff, wide = down_weight.shape[1:]
    per = cfg.sources * cfg.cap

    z, c, t = (lax.axis_index(a) for a in ("expert", "context", "tensor"))
    pos = jnp.stack([z, c, t]).astype(I32)
    ids = expert_ids.reshape(1, n)
    route = route_weights.reshape(1, n)
    smem = pl.BlockSpec(memory_space=pltpu.SMEM)
    vmem = pl.BlockSpec(memory_space=pltpu.VMEM)
    params = pltpu.CompilerParams(vmem_limit_bytes=VMEM_LIMIT)
    shape = jax.ShapeDtypeStruct

    def call(kernel, name, ins, outs, scratch=(), work=10**9):
        args = [pos] + list(ins)
        return list(pl.pallas_call(
            kernel, in_specs=[smem] + [vmem] * len(ins), out_specs=[vmem] * len(outs),
            out_shape=[o if isinstance(o, shape) else shape(o, BF16) for o in outs], scratch_shapes=scratch, compiler_params=params, name=name,
            cost_estimate=pl.CostEstimate(flops=work, bytes_accessed=0, transcendentals=0))(*args))

    def kernel(f):
        return functools.partial(f, cfg)

    blocks = call(kernel(dispatch_kernel), "dispatch", [ids, tokens], [(cfg.rp, cfg.w)] * cfg.groups, work=LEAD)

    def move(x, r, dc):
        return lax.ppermute(x, ("expert", "context"), [
            (i * 2 + k, (i ^ r) * 2 + (k ^ dc)) for i in range(cfg.groups) for k in range(2)])

    half = cfg.ne // 2
    early, late = cfg.early * 32, (cfg.groups - cfg.early) * 32
    held = [blocks[0]] + [move(blocks[r], r, 0) for r in range(1, cfg.groups)]
    crossed = [swap(x, "context") for x in held]


    def four(r):
        return [held[r], swap(held[r], "tensor"), crossed[r], swap(crossed[r], "tensor")]

    near, info = call(kernel(near_kernel), "near", [b for r in cfg.visits[:cfg.early] for b in four(r)] + [ids, route],
                      [(cfg.ne, early, width), shape((2, n), F32)])
    info_peer = swap(info, "tensor")
    far = [b for r in cfg.visits[cfg.early:] for b in four(r)]
    hid_a, later = call(kernel(hidden_first_kernel), "hidden_a", far + [near, gate_weight, up_weight],
                        [(half * per, f), (half, late, width)], [pltpu.VMEM((half, late, width), BF16)], work=STEP)
    xa = swap(hid_a, "context")
    hid_b = call(kernel(hidden_second_kernel), "hidden_b", [near, later, gate_weight, up_weight],
                 [(half * per, f)], work=STEP)[0]
    xb = swap(hid_b, "context")
    full = pltpu.VMEM((half * per, ff), BF16)
    out_a = call(kernel(down_first_kernel), "down_a", [hid_a, xa, swap(hid_a, "tensor"), swap(xa, "tensor"), down_weight, info_peer],
                 [(half * per, wide)], [full], work=STEP)[0]
    message = (4 * cfg.rows, wide // 2)
    outs = call(
        kernel(down_second_kernel), "down_b",
        [hid_b, xb, swap(hid_b, "tensor"), swap(xb, "tensor"), down_weight, out_a],
        [message] * (cfg.groups * 2), [full, pltpu.VMEM((half * per, wide), BF16)], work=STEP)
    returned = [outs[0]] + [move(o, k // 2, k % 2) for k, o in enumerate(outs) if k]
    order = ORDER
    mine, other = call(
        lambda pos_ref, own, peer, *refs: combine_kernel(
            cfg, pos_ref, own, peer, *[refs[order.index(k)] for k in range(len(order))], *refs[len(order):]),
        "combine", [info, info_peer] + [returned[k] for k in order], [(n, 2 * wide)] * 2)
    return call(kernel(join_kernel), "join", [mine, swap(other, "tensor")], [(n, width)])[0]


def by_gathers(tokens, expert_ids, route_weights, gate_weight, up_weight, down_weight):
    n, width = tokens.shape
    local = gate_weight.shape[0]
    groups = lax.axis_size("expert")
    experts = local * groups
    cap = max(2, n * 5 // (4 * experts))
    ids = expert_ids[:, 0]
    member = (ids[:, None] == jnp.arange(experts, dtype=I32)[None, :]).astype(I32)
    rank = jnp.sum((jnp.cumsum(member, axis=0) - 1) * member, axis=1)
    key = ids * cap + rank
    pick = onehot(key[:, None] == jnp.arange(experts * cap, dtype=I32)[None, :])
    out = jnp.dot(pick.T, tokens, preferred_element_type=F32).astype(BF16)
    out = out.reshape(groups, local, cap, width).transpose(1, 0, 2, 3)
    inc = lax.all_to_all(out, "expert", split_axis=1, concat_axis=1, tiled=True)
    inc = inc.reshape(local, groups * cap, width)
    rows = lax.all_gather(inc, ("context", "tensor"), axis=1, tiled=True)
    g = jnp.einsum("end,edf->enf", rows, gate_weight, preferred_element_type=F32)
    u = jnp.einsum("end,edf->enf", rows, up_weight, preferred_element_type=F32)
    hid = (jax.nn.silu(g) * u).astype(BF16)
    hid = lax.all_gather(hid, ("context", "tensor"), axis=2, tiled=True)
    res = jnp.einsum("erf,efd->erd", hid, down_weight, preferred_element_type=F32).astype(BF16)
    back = lax.all_to_all(res, ("context", "tensor"), split_axis=1, concat_axis=2, tiled=True)
    back = back.reshape(local, groups, cap, width)
    back = lax.all_to_all(back, "expert", split_axis=1, concat_axis=1, tiled=True)
    back = back.transpose(1, 0, 2, 3).reshape(experts * cap, width)
    picked = jnp.dot(pick, back, preferred_element_type=F32)
    return (route_weights * picked).astype(BF16)


def solution(mesh):
    size = dict(mesh.shape)
    paired = size["context"] == 2 and size["tensor"] == 2 and size["expert"] == 4
    rows = P(("group", "expert", "context", "tensor"), None)
    weights = P("expert", None, ("context", "tensor"))
    return jax.shard_map(
        on_device if paired else by_gathers,
        mesh=mesh,
        in_specs=(rows, rows, rows, weights, weights, weights),
        out_specs=rows,
        check_vma=False,
    )
```

```python
import functools
import jax
import jax.numpy as jnp
from jax import lax
from jax.experimental import pallas as pl
from jax.experimental.pallas import tpu as pltpu
from jax.sharding import PartitionSpec as P

BIG = 4096
ORDER = (0, 4, 1, 5, 3, 6, 7, 2)
LEAD = 20 * 10**9
STEP = 10 * 10**9
VMEM_LIMIT = 8 * 1024 * 1024
F32, BF16, I32 = jnp.float32, jnp.bfloat16, jnp.int32


def div(x, by):
    return ((x.astype(F32) + 0.5) * (1.0 / by)).astype(I32)


def onehot(cond):
    return jnp.where(cond, 1.0, 0.0).astype(BF16)


def dot(a, b):
    return jnp.dot(a, b, preferred_element_type=F32)


def iota(shape, dim):
    return lax.broadcasted_iota(I32, shape, dim)


def as_column(row):
    n = row.shape[1]
    square = jnp.broadcast_to(row, (n, n))
    return jnp.sum(jnp.where(iota((n, n), 0) == iota((n, n), 1), square, jnp.zeros((), row.dtype)), axis=1, keepdims=True)


def slot_keys(ids_row, cap):
    n = ids_row.shape[1]
    ids_col = as_column(ids_row)
    earlier = (ids_col == ids_row) & (iota((n, n), 0) < iota((n, n), 1))
    rank = jnp.sum(jnp.where(earlier, 1, 0), axis=0, keepdims=True)
    return ids_row * cap + rank


def dispatch_kernel(cfg, pos_ref, ids_ref, tok_ref, *outs):
    z = pos_ref[0]
    keys = slot_keys(ids_ref[...], cfg.cap)
    keys = jnp.concatenate([keys + j * BIG for j in range(cfg.nd)], axis=1)
    stacked = jnp.concatenate([tok_ref[:, j * cfg.w:(j + 1) * cfg.w] for j in range(cfg.nd)], axis=0)
    i = iota((cfg.rp, 1), 0)
    j = div(i, cfg.rows)
    target = i - j * cfg.rows + j * BIG
    for r in range(cfg.groups):
        base = jnp.bitwise_xor(z, r) * cfg.local * cfg.cap
        outs[r][...] = dot(onehot(keys - base == target), stacked).astype(BF16)


def place(cfg, srcs, store):
    i, c = iota((cfg.nd * cfg.ne * 16, 1), 0), iota((1, 2 * cfg.rp), 1)
    slot = i & 7
    want = ((i >> 3) & 1) * cfg.rp + (i >> 4) * cfg.cap + slot
    spread = onehot((want == c) & (slot < cfg.cap))
    for k in range(len(srcs) // 2):
        pair = jnp.concatenate([srcs[2 * k][...], srcs[2 * k + 1][...]], axis=0)
        spaced = dot(spread, pair).astype(BF16)
        for j in range(cfg.nd):
            for e in range(cfg.ne):
                at = (j * cfg.ne + e) * 16
                store(e, k, j, spaced[at:at + 16])


def near_kernel(cfg, pos_ref, *refs):
    ids_ref, route_ref, rows, info = refs[-4:]
    info[0:1] = slot_keys(ids_ref[...], cfg.cap).astype(F32)
    info[1:2] = route_ref[...]

    def store(e, k, j, v):
        rows[e, k * 16:(k + 1) * 16, j * cfg.w:(j + 1) * cfg.w] = v

    place(cfg, refs[:cfg.early * 4], store)


def hidden_rows(cfg, pos_ref, near, far, gate, up, out_ref, first):
    per = cfg.sources * cfg.cap
    i = iota((per, 1), 0)
    s = div(i, cfg.cap)
    slot = i - s * cfg.cap
    rel = jnp.bitwise_xor(s & 3, pos_ref[1] * 2 + pos_ref[2])
    for k, r in enumerate(cfg.visits):
        rel = rel + jnp.where((s >> 2) == r, 4 * k, 0)
    compact = onehot(iota((1, cfg.sources * 8), 1) == rel * 8 + slot)
    for k in range(cfg.ne // 2):
        e = first + k
        x = jnp.concatenate([near[e], far[k]], axis=0)
        both = dot(x, jnp.concatenate([gate[e], up[e]], axis=1))
        g, u = jnp.split(both, 2, axis=1)
        hid = (g / (1.0 + jnp.exp(-g)) * u).astype(BF16)
        out_ref[k * per:(k + 1) * per] = dot(compact, hid).astype(BF16)


def hidden_first_kernel(cfg, pos_ref, *refs):
    late = cfg.sources - cfg.early * 4
    near, gate, up, out_ref, later, now = refs[late:]

    def store(e, k, j, v):
        ref = now if e < cfg.ne // 2 else later
        ref[e % (cfg.ne // 2), k * 16:(k + 1) * 16, j * cfg.w:(j + 1) * cfg.w] = v

    place(cfg, refs[:late], store)
    hidden_rows(cfg, pos_ref, near, now, gate, up, out_ref, 0)


def hidden_second_kernel(cfg, pos_ref, near, far, gate, up, out_ref):
    hidden_rows(cfg, pos_ref, near, far, gate, up, out_ref, cfg.ne // 2)


def down_rows(cfg, pos_ref, parts, down, full, out, first):
    c, t = pos_ref[1], pos_ref[2]
    f = parts[0].shape[1]
    for ref, dc, dt in zip(parts, (0, 1, 0, 1), (0, 0, 1, 1)):
        at = (jnp.bitwise_xor(c, dc) * 2 + jnp.bitwise_xor(t, dt)) * f
        full[:, pl.ds(pl.multiple_of(at, 128), f)] = ref[...]
    per = cfg.sources * cfg.cap
    for k in range(cfg.ne // 2):
        out[k * per:(k + 1) * per] = dot(full[k * per:(k + 1) * per], down[first + k]).astype(BF16)


def sort_rows(cfg, pos_ref, halves, outs):
    per = cfg.sources * cfg.cap
    width = halves[0].shape[1] // 2
    stacked = jnp.concatenate([v[:, q * width:(q + 1) * width] for q in range(2) for v in halves], axis=0)
    m = iota((4 * cfg.rows, 1), 0)
    qt = div(m, cfg.rows)
    p = m - qt * cfg.rows
    e = div(p, cfg.cap)
    slot = p - e * cfg.cap
    want = (qt >> 1) * (cfg.ne * per) + e * per + (qt & 1) * cfg.cap + slot
    lane = iota((1, 2 * cfg.ne * per), 1)
    for k, out in enumerate(outs):
        r, dc = divmod(k, 2)
        place_at = (r * 2 + jnp.bitwise_xor(pos_ref[1], dc)) * 2 * cfg.cap
        out[...] = dot(onehot(lane - place_at == want), stacked).astype(BF16)


def down_first_kernel(cfg, pos_ref, own, x, core, xcore, down, info, out, full):
    down_rows(cfg, pos_ref, (own, x, core, xcore), down, full, out, 0)


def down_second_kernel(cfg, pos_ref, own, x, core, xcore, down, before, *refs):
    outs, full, out = refs[:-2], refs[-2], refs[-1]
    down_rows(cfg, pos_ref, (own, x, core, xcore), down, full, out, cfg.ne // 2)
    sort_rows(cfg, pos_ref, (before, out), outs)


def combine_kernel(cfg, pos_ref, info_own, info_peer, *refs):
    msgs, (mine, other) = refs[:-2], refs[-2:]
    z, c, t = pos_ref[0], pos_ref[1], pos_ref[2]
    block = 4 * cfg.rows
    lanes = iota((1, cfg.groups * block), 1)
    r = div(lanes, block)
    m = lanes - r * block
    qt = div(m, cfg.rows)
    code = jnp.bitwise_xor(r, z) * cfg.local * cfg.cap + m - qt * cfg.rows + qt * BIG
    picks, weights = [], []
    for rel, info in enumerate((info_own, info_peer)):
        key = as_column(info[0:1]).astype(I32)
        weights.append(as_column(info[1:2]))
        picks += [onehot(key + (q * 2 + jnp.bitwise_xor(t, rel)) * BIG == code) for q in range(2)]
    picks = jnp.concatenate(picks, axis=0)
    n = info_own.shape[1]
    for dc in range(2):
        stacked = jnp.concatenate([msgs[k * 2 + dc][...] for k in range(cfg.groups)], axis=0)
        got = dot(picks, stacked)
        width = got.shape[1]
        at = jnp.bitwise_xor(c, dc) * (2 * width)
        for rel, out in enumerate((mine, other)):
            for q in range(2):
                k = rel * 2 + q
                out[:, pl.ds(pl.multiple_of(at + q * width, 128), width)] = (weights[rel] * got[k * n:(k + 1) * n]).astype(BF16)


def join_kernel(cfg, pos_ref, mine, other, out):
    t = pos_ref[2]
    width = mine.shape[1] // 2
    for cc in range(2):
        for ref, dt in ((mine, 0), (other, 1)):
            at = cc * 2 * width + jnp.bitwise_xor(t, dt) * width
            out[:, pl.ds(pl.multiple_of(at, 128), width)] = ref[:, cc * width:(cc + 1) * width]


class Sizes:
    pass


def swap(x, axis):
    return lax.ppermute(x, axis, [(0, 1), (1, 0)])


def on_device(tokens, expert_ids, route_weights, gate_weight, up_weight, down_weight):
    cfg = Sizes()
    n, width = tokens.shape
    cfg.groups = lax.axis_size("expert")
    cfg.local = gate_weight.shape[0]
    experts = cfg.groups * cfg.local
    cfg.cap = max(2, n * 5 // (4 * experts))
    cfg.ne = cfg.local
    cfg.rows = cfg.ne * cfg.cap
    cfg.nd = 16 // cfg.ne
    cfg.w = width // cfg.nd
    cfg.rp = cfg.rows * cfg.nd
    cfg.sources = cfg.groups * 4
    cfg.early = 3
    cfg.visits = (0, 1, 3, 2)
    f = gate_weight.shape[2]
    ff, wide = down_weight.shape[1:]
    per = cfg.sources * cfg.cap

    z, c, t = (lax.axis_index(a) for a in ("expert", "context", "tensor"))
    pos = jnp.stack([z, c, t]).astype(I32)
    ids = expert_ids.reshape(1, n)
    route = route_weights.reshape(1, n)
    smem = pl.BlockSpec(memory_space=pltpu.SMEM)
    vmem = pl.BlockSpec(memory_space=pltpu.VMEM)
    params = pltpu.CompilerParams(vmem_limit_bytes=VMEM_LIMIT)
    shape = jax.ShapeDtypeStruct

    def call(kernel, name, ins, outs, scratch=(), work=10**9):
        args = [pos] + list(ins)
        return list(pl.pallas_call(
            kernel, in_specs=[smem] + [vmem] * len(ins), out_specs=[vmem] * len(outs),
            out_shape=[o if isinstance(o, shape) else shape(o, BF16) for o in outs], scratch_shapes=scratch, compiler_params=params, name=name,
            cost_estimate=pl.CostEstimate(flops=work, bytes_accessed=0, transcendentals=0))(*args))

    def kernel(f):
        return functools.partial(f, cfg)

    blocks = call(kernel(dispatch_kernel), "dispatch", [ids, tokens], [(cfg.rp, cfg.w)] * cfg.groups, work=LEAD)

    def move(x, r, dc):
        return lax.ppermute(x, ("expert", "context"), [
            (i * 2 + k, (i ^ r) * 2 + (k ^ dc)) for i in range(cfg.groups) for k in range(2)])

    half = cfg.ne // 2
    early, late = cfg.early * 32, (cfg.groups - cfg.early) * 32
    held = [blocks[0]] + [move(blocks[r], r, 0) for r in range(1, cfg.groups)]
    crossed = [swap(x, "context") for x in held]


    def four(r):
        return [held[r], swap(held[r], "tensor"), crossed[r], swap(crossed[r], "tensor")]

    near, info = call(kernel(near_kernel), "near", [b for r in cfg.visits[:cfg.early] for b in four(r)] + [ids, route],
                      [(cfg.ne, early, width), shape((2, n), F32)])
    info_peer = swap(info, "tensor")
    far = [b for r in cfg.visits[cfg.early:] for b in four(r)]
    hid_a, later = call(kernel(hidden_first_kernel), "hidden_a", far + [near, gate_weight, up_weight],
                        [(half * per, f), (half, late, width)], [pltpu.VMEM((half, late, width), BF16)], work=STEP)
    xa = swap(hid_a, "context")
    hid_b = call(kernel(hidden_second_kernel), "hidden_b", [near, later, gate_weight, up_weight],
                 [(half * per, f)], work=STEP)[0]
    xb = swap(hid_b, "context")
    full = pltpu.VMEM((half * per, ff), BF16)
    out_a = call(kernel(down_first_kernel), "down_a", [hid_a, xa, swap(hid_a, "tensor"), swap(xa, "tensor"), down_weight, info_peer],
                 [(half * per, wide)], [full], work=STEP)[0]
    message = (4 * cfg.rows, wide // 2)
    outs = call(
        kernel(down_second_kernel), "down_b",
        [hid_b, xb, swap(hid_b, "tensor"), swap(xb, "tensor"), down_weight, out_a],
        [message] * (cfg.groups * 2), [full, pltpu.VMEM((half * per, wide), BF16)], work=STEP)
    returned = [outs[0]] + [move(o, k // 2, k % 2) for k, o in enumerate(outs) if k]
    order = ORDER
    mine, other = call(
        lambda pos_ref, own, peer, *refs: combine_kernel(
            cfg, pos_ref, own, peer, *[refs[order.index(k)] for k in range(len(order))], *refs[len(order):]),
        "combine", [info, info_peer] + [returned[k] for k in order], [(n, 2 * wide)] * 2)
    return call(kernel(join_kernel), "join", [mine, swap(other, "tensor")], [(n, width)])[0]


def by_gathers(tokens, expert_ids, route_weights, gate_weight, up_weight, down_weight):
    n, width = tokens.shape
    local = gate_weight.shape[0]
    groups = lax.axis_size("expert")
    experts = local * groups
    cap = max(2, n * 5 // (4 * experts))
    ids = expert_ids[:, 0]
    member = (ids[:, None] == jnp.arange(experts, dtype=I32)[None, :]).astype(I32)
    rank = jnp.sum((jnp.cumsum(member, axis=0) - 1) * member, axis=1)
    key = ids * cap + rank
    pick = onehot(key[:, None] == jnp.arange(experts * cap, dtype=I32)[None, :])
    out = jnp.dot(pick.T, tokens, preferred_element_type=F32).astype(BF16)
    out = out.reshape(groups, local, cap, width).transpose(1, 0, 2, 3)
    inc = lax.all_to_all(out, "expert", split_axis=1, concat_axis=1, tiled=True)
    inc = inc.reshape(local, groups * cap, width)
    rows = lax.all_gather(inc, ("context", "tensor"), axis=1, tiled=True)
    g = jnp.einsum("end,edf->enf", rows, gate_weight, preferred_element_type=F32)
    u = jnp.einsum("end,edf->enf", rows, up_weight, preferred_element_type=F32)
    hid = (jax.nn.silu(g) * u).astype(BF16)
    hid = lax.all_gather(hid, ("context", "tensor"), axis=2, tiled=True)
    res = jnp.einsum("erf,efd->erd", hid, down_weight, preferred_element_type=F32).astype(BF16)
    back = lax.all_to_all(res, ("context", "tensor"), split_axis=1, concat_axis=2, tiled=True)
    back = back.reshape(local, groups, cap, width)
    back = lax.all_to_all(back, "expert", split_axis=1, concat_axis=1, tiled=True)
    back = back.transpose(1, 0, 2, 3).reshape(experts * cap, width)
    picked = jnp.dot(pick, back, preferred_element_type=F32)
    return (route_weights * picked).astype(BF16)


def solution(mesh):
    size = dict(mesh.shape)
    paired = size["context"] == 2 and size["tensor"] == 2 and size["expert"] == 4
    rows = P(("group", "expert", "context", "tensor"), None)
    weights = P("expert", None, ("context", "tensor"))
    return jax.shard_map(
        on_device if paired else by_gathers,
        mesh=mesh,
        in_specs=(rows, rows, rows, weights, weights, weights),
        out_specs=rows,
        check_vma=False,
    )
```

```python
import functools
import jax
import jax.numpy as jnp
from jax import lax
from jax.experimental import pallas as pl
from jax.experimental.pallas import tpu as pltpu
from jax.sharding import PartitionSpec as P

BIG = 4096
ORDER = (0, 4, 3, 5, 1, 6, 7, 2)
LEAD = 20 * 10**9
STEP = 10 * 10**9
VMEM_LIMIT = 8 * 1024 * 1024
F32, BF16, I32 = jnp.float32, jnp.bfloat16, jnp.int32


def div(x, by):
    return ((x.astype(F32) + 0.5) * (1.0 / by)).astype(I32)


def onehot(cond):
    return jnp.where(cond, 1.0, 0.0).astype(BF16)


def dot(a, b):
    return jnp.dot(a, b, preferred_element_type=F32)


def iota(shape, dim):
    return lax.broadcasted_iota(I32, shape, dim)


def as_column(row):
    n = row.shape[1]
    square = jnp.broadcast_to(row, (n, n))
    return jnp.sum(jnp.where(iota((n, n), 0) == iota((n, n), 1), square, jnp.zeros((), row.dtype)), axis=1, keepdims=True)


def slot_keys(ids_row, cap):
    n = ids_row.shape[1]
    ids_col = as_column(ids_row)
    earlier = (ids_col == ids_row) & (iota((n, n), 0) < iota((n, n), 1))
    rank = jnp.sum(jnp.where(earlier, 1, 0), axis=0, keepdims=True)
    return ids_row * cap + rank


def dispatch_kernel(cfg, pos_ref, ids_ref, tok_ref, *outs):
    z = pos_ref[0]
    keys = slot_keys(ids_ref[...], cfg.cap)
    keys = jnp.concatenate([keys + j * BIG for j in range(cfg.nd)], axis=1)
    stacked = jnp.concatenate([tok_ref[:, j * cfg.w:(j + 1) * cfg.w] for j in range(cfg.nd)], axis=0)
    i = iota((cfg.rp, 1), 0)
    j = div(i, cfg.rows)
    target = i - j * cfg.rows + j * BIG
    for r in range(cfg.groups):
        base = jnp.bitwise_xor(z, r) * cfg.local * cfg.cap
        outs[r][...] = dot(onehot(keys - base == target), stacked).astype(BF16)


def place(cfg, srcs, store):
    i, c = iota((cfg.nd * cfg.ne * 16, 1), 0), iota((1, 2 * cfg.rp), 1)
    slot = i & 7
    want = ((i >> 3) & 1) * cfg.rp + (i >> 4) * cfg.cap + slot
    spread = onehot((want == c) & (slot < cfg.cap))
    for k in range(len(srcs) // 2):
        pair = jnp.concatenate([srcs[2 * k][...], srcs[2 * k + 1][...]], axis=0)
        spaced = dot(spread, pair).astype(BF16)
        for j in range(cfg.nd):
            for e in range(cfg.ne):
                at = (j * cfg.ne + e) * 16
                store(e, k, j, spaced[at:at + 16])


def near_kernel(cfg, pos_ref, *refs):
    ids_ref, route_ref, rows, info = refs[-4:]
    info[0:1] = slot_keys(ids_ref[...], cfg.cap).astype(F32)
    info[1:2] = route_ref[...]

    def store(e, k, j, v):
        rows[e, k * 16:(k + 1) * 16, j * cfg.w:(j + 1) * cfg.w] = v

    place(cfg, refs[:cfg.early * 4], store)


def hidden_rows(cfg, pos_ref, near, far, gate, up, out_ref, first):
    per = cfg.sources * cfg.cap
    i = iota((per, 1), 0)
    s = div(i, cfg.cap)
    slot = i - s * cfg.cap
    rel = jnp.bitwise_xor(s & 3, pos_ref[1] * 2 + pos_ref[2])
    for k, r in enumerate(cfg.visits):
        rel = rel + jnp.where((s >> 2) == r, 4 * k, 0)
    compact = onehot(iota((1, cfg.sources * 8), 1) == rel * 8 + slot)
    for k in range(cfg.ne // 2):
        e = first + k
        x = jnp.concatenate([near[e], far[k]], axis=0)
        both = dot(x, jnp.concatenate([gate[e], up[e]], axis=1))
        g, u = jnp.split(both, 2, axis=1)
        hid = (g / (1.0 + jnp.exp(-g)) * u).astype(BF16)
        out_ref[k * per:(k + 1) * per] = dot(compact, hid).astype(BF16)


def hidden_first_kernel(cfg, pos_ref, *refs):
    late = cfg.sources - cfg.early * 4
    near, gate, up, out_ref, later, now = refs[late:]

    def store(e, k, j, v):
        ref = now if e < cfg.ne // 2 else later
        ref[e % (cfg.ne // 2), k * 16:(k + 1) * 16, j * cfg.w:(j + 1) * cfg.w] = v

    place(cfg, refs[:late], store)
    hidden_rows(cfg, pos_ref, near, now, gate, up, out_ref, 0)


def hidden_second_kernel(cfg, pos_ref, near, far, gate, up, out_ref):
    hidden_rows(cfg, pos_ref, near, far, gate, up, out_ref, cfg.ne // 2)


def down_rows(cfg, pos_ref, parts, down, full, out, first):
    c, t = pos_ref[1], pos_ref[2]
    f = parts[0].shape[1]
    for ref, dc, dt in zip(parts, (0, 1, 0, 1), (0, 0, 1, 1)):
        at = (jnp.bitwise_xor(c, dc) * 2 + jnp.bitwise_xor(t, dt)) * f
        full[:, pl.ds(pl.multiple_of(at, 128), f)] = ref[...]
    per = cfg.sources * cfg.cap
    for k in range(cfg.ne // 2):
        out[k * per:(k + 1) * per] = dot(full[k * per:(k + 1) * per], down[first + k]).astype(BF16)


def sort_rows(cfg, pos_ref, halves, outs):
    per = cfg.sources * cfg.cap
    width = halves[0].shape[1] // 2
    stacked = jnp.concatenate([v[:, q * width:(q + 1) * width] for q in range(2) for v in halves], axis=0)
    m = iota((4 * cfg.rows, 1), 0)
    qt = div(m, cfg.rows)
    p = m - qt * cfg.rows
    e = div(p, cfg.cap)
    slot = p - e * cfg.cap
    want = (qt >> 1) * (cfg.ne * per) + e * per + (qt & 1) * cfg.cap + slot
    lane = iota((1, 2 * cfg.ne * per), 1)
    for k, out in enumerate(outs):
        r, dc = divmod(k, 2)
        place_at = (r * 2 + jnp.bitwise_xor(pos_ref[1], dc)) * 2 * cfg.cap
        out[...] = dot(onehot(lane - place_at == want), stacked).astype(BF16)


def down_first_kernel(cfg, pos_ref, own, x, core, xcore, down, info, out, full):
    down_rows(cfg, pos_ref, (own, x, core, xcore), down, full, out, 0)


def down_second_kernel(cfg, pos_ref, own, x, core, xcore, down, before, *refs):
    outs, full, out = refs[:-2], refs[-2], refs[-1]
    down_rows(cfg, pos_ref, (own, x, core, xcore), down, full, out, cfg.ne // 2)
    sort_rows(cfg, pos_ref, (before, out), outs)


def combine_kernel(cfg, pos_ref, info_own, info_peer, *refs):
    msgs, (mine, other) = refs[:-2], refs[-2:]
    z, c, t = pos_ref[0], pos_ref[1], pos_ref[2]
    block = 4 * cfg.rows
    lanes = iota((1, cfg.groups * block), 1)
    r = div(lanes, block)
    m = lanes - r * block
    qt = div(m, cfg.rows)
    code = jnp.bitwise_xor(r, z) * cfg.local * cfg.cap + m - qt * cfg.rows + qt * BIG
    picks, weights = [], []
    for rel, info in enumerate((info_own, info_peer)):
        key = as_column(info[0:1]).astype(I32)
        weights.append(as_column(info[1:2]))
        picks += [onehot(key + (q * 2 + jnp.bitwise_xor(t, rel)) * BIG == code) for q in range(2)]
    picks = jnp.concatenate(picks, axis=0)
    n = info_own.shape[1]
    for dc in range(2):
        stacked = jnp.concatenate([msgs[k * 2 + dc][...] for k in range(cfg.groups)], axis=0)
        got = dot(picks, stacked)
        width = got.shape[1]
        at = jnp.bitwise_xor(c, dc) * (2 * width)
        for rel, out in enumerate((mine, other)):
            for q in range(2):
                k = rel * 2 + q
                out[:, pl.ds(pl.multiple_of(at + q * width, 128), width)] = (weights[rel] * got[k * n:(k + 1) * n]).astype(BF16)


class Sizes:
    pass


def swap(x, axis):
    return lax.ppermute(x, axis, [(0, 1), (1, 0)])


def on_device(tokens, expert_ids, route_weights, gate_weight, up_weight, down_weight):
    cfg = Sizes()
    n, width = tokens.shape
    cfg.groups = lax.axis_size("expert")
    cfg.local = gate_weight.shape[0]
    experts = cfg.groups * cfg.local
    cfg.cap = max(2, n * 5 // (4 * experts))
    cfg.ne = cfg.local
    cfg.rows = cfg.ne * cfg.cap
    cfg.nd = 16 // cfg.ne
    cfg.w = width // cfg.nd
    cfg.rp = cfg.rows * cfg.nd
    cfg.sources = cfg.groups * 4
    cfg.early = 3
    cfg.visits = (0, 1, 3, 2)
    f = gate_weight.shape[2]
    ff, wide = down_weight.shape[1:]
    per = cfg.sources * cfg.cap

    z, c, t = (lax.axis_index(a) for a in ("expert", "context", "tensor"))
    pos = jnp.stack([z, c, t]).astype(I32)
    ids = expert_ids.reshape(1, n)
    route = route_weights.reshape(1, n)
    smem = pl.BlockSpec(memory_space=pltpu.SMEM)
    vmem = pl.BlockSpec(memory_space=pltpu.VMEM)
    params = pltpu.CompilerParams(vmem_limit_bytes=VMEM_LIMIT)
    shape = jax.ShapeDtypeStruct

    def call(kernel, name, ins, outs, scratch=(), work=10**9):
        args = [pos] + list(ins)
        return list(pl.pallas_call(
            kernel, in_specs=[smem] + [vmem] * len(ins), out_specs=[vmem] * len(outs),
            out_shape=[o if isinstance(o, shape) else shape(o, BF16) for o in outs], scratch_shapes=scratch, compiler_params=params, name=name,
            cost_estimate=pl.CostEstimate(flops=work, bytes_accessed=0, transcendentals=0))(*args))

    def kernel(f):
        return functools.partial(f, cfg)

    blocks = call(kernel(dispatch_kernel), "dispatch", [ids, tokens], [(cfg.rp, cfg.w)] * cfg.groups, work=LEAD)

    def move(x, r, dc):
        return lax.ppermute(x, ("expert", "context"), [
            (i * 2 + k, (i ^ r) * 2 + (k ^ dc)) for i in range(cfg.groups) for k in range(2)])

    half = cfg.ne // 2
    early, late = cfg.early * 32, (cfg.groups - cfg.early) * 32
    held = [blocks[0]] + [move(blocks[r], r, 0) for r in range(1, cfg.groups)]
    crossed = [swap(x, "context") for x in held]


    def four(r):
        return [held[r], swap(held[r], "tensor"), crossed[r], swap(crossed[r], "tensor")]

    near, info = call(kernel(near_kernel), "near", [b for r in cfg.visits[:cfg.early] for b in four(r)] + [ids, route],
                      [(cfg.ne, early, width), shape((2, n), F32)])
    info_peer = swap(info, "tensor")
    far = [b for r in cfg.visits[cfg.early:] for b in four(r)]
    hid_a, later = call(kernel(hidden_first_kernel), "hidden_a", far + [near, gate_weight, up_weight],
                        [(half * per, f), (half, late, width)], [pltpu.VMEM((half, late, width), BF16)], work=STEP)
    xa = swap(hid_a, "context")
    hid_b = call(kernel(hidden_second_kernel), "hidden_b", [near, later, gate_weight, up_weight],
                 [(half * per, f)], work=STEP)[0]
    xb = swap(hid_b, "context")
    full = pltpu.VMEM((half * per, ff), BF16)
    out_a = call(kernel(down_first_kernel), "down_a", [hid_a, xa, swap(hid_a, "tensor"), swap(xa, "tensor"), down_weight, info_peer],
                 [(half * per, wide)], [full], work=STEP)[0]
    message = (4 * cfg.rows, wide // 2)
    outs = call(
        kernel(down_second_kernel), "down_b",
        [hid_b, xb, swap(hid_b, "tensor"), swap(xb, "tensor"), down_weight, out_a],
        [message] * (cfg.groups * 2), [full, pltpu.VMEM((half * per, wide), BF16)], work=STEP)
    returned = [outs[0]] + [move(o, k // 2, k % 2) for k, o in enumerate(outs) if k]
    order = ORDER
    mine, other = call(
        lambda pos_ref, own, peer, *refs: combine_kernel(
            cfg, pos_ref, own, peer, *[refs[order.index(k)] for k in range(len(order))], *refs[len(order):]),
        "combine", [info, info_peer] + [returned[k] for k in order], [(n, 2 * wide)] * 2)
    received = swap(other, "tensor")
    first, second = jnp.where(t == 0, mine, received), jnp.where(t == 0, received, mine)
    return jnp.concatenate([first[:, :wide], second[:, :wide], first[:, wide:], second[:, wide:]], axis=1)


def by_gathers(tokens, expert_ids, route_weights, gate_weight, up_weight, down_weight):
    n, width = tokens.shape
    local = gate_weight.shape[0]
    groups = lax.axis_size("expert")
    experts = local * groups
    cap = max(2, n * 5 // (4 * experts))
    ids = expert_ids[:, 0]
    member = (ids[:, None] == jnp.arange(experts, dtype=I32)[None, :]).astype(I32)
    rank = jnp.sum((jnp.cumsum(member, axis=0) - 1) * member, axis=1)
    key = ids * cap + rank
    pick = onehot(key[:, None] == jnp.arange(experts * cap, dtype=I32)[None, :])
    out = jnp.dot(pick.T, tokens, preferred_element_type=F32).astype(BF16)
    out = out.reshape(groups, local, cap, width).transpose(1, 0, 2, 3)
    inc = lax.all_to_all(out, "expert", split_axis=1, concat_axis=1, tiled=True)
    inc = inc.reshape(local, groups * cap, width)
    rows = lax.all_gather(inc, ("context", "tensor"), axis=1, tiled=True)
    g = jnp.einsum("end,edf->enf", rows, gate_weight, preferred_element_type=F32)
    u = jnp.einsum("end,edf->enf", rows, up_weight, preferred_element_type=F32)
    hid = (jax.nn.silu(g) * u).astype(BF16)
    hid = lax.all_gather(hid, ("context", "tensor"), axis=2, tiled=True)
    res = jnp.einsum("erf,efd->erd", hid, down_weight, preferred_element_type=F32).astype(BF16)
    back = lax.all_to_all(res, ("context", "tensor"), split_axis=1, concat_axis=2, tiled=True)
    back = back.reshape(local, groups, cap, width)
    back = lax.all_to_all(back, "expert", split_axis=1, concat_axis=1, tiled=True)
    back = back.transpose(1, 0, 2, 3).reshape(experts * cap, width)
    picked = jnp.dot(pick, back, preferred_element_type=F32)
    return (route_weights * picked).astype(BF16)


def solution(mesh):
    size = dict(mesh.shape)
    paired = size["context"] == 2 and size["tensor"] == 2 and size["expert"] == 4
    rows = P(("group", "expert", "context", "tensor"), None)
    weights = P("expert", None, ("context", "tensor"))
    return jax.shard_map(
        on_device if paired else by_gathers,
        mesh=mesh,
        in_specs=(rows, rows, rows, weights, weights, weights),
        out_specs=rows,
        check_vma=False,
    )
```

```python
import functools
import jax
import jax.numpy as jnp
from jax import lax
from jax.experimental import pallas as pl
from jax.experimental.pallas import tpu as pltpu
from jax.sharding import PartitionSpec as P

BIG = 4096
ORDER = (0, 4, 3, 5, 1, 6, 7, 2)
LEAD = 20 * 10**9
STEP = 10 * 10**9
VMEM_LIMIT = 8 * 1024 * 1024
F32, BF16, I32 = jnp.float32, jnp.bfloat16, jnp.int32


def div(x, by):
    return ((x.astype(F32) + 0.5) * (1.0 / by)).astype(I32)


def onehot(cond):
    return jnp.where(cond, 1.0, 0.0).astype(BF16)


def dot(a, b):
    return jnp.dot(a, b, preferred_element_type=F32)


def iota(shape, dim):
    return lax.broadcasted_iota(I32, shape, dim)


def as_column(row):
    n = row.shape[1]
    square = jnp.broadcast_to(row, (n, n))
    return jnp.sum(jnp.where(iota((n, n), 0) == iota((n, n), 1), square, jnp.zeros((), row.dtype)), axis=1, keepdims=True)


def slot_keys(ids_row, cap):
    n = ids_row.shape[1]
    ids_col = as_column(ids_row)
    earlier = (ids_col == ids_row) & (iota((n, n), 0) < iota((n, n), 1))
    rank = jnp.sum(jnp.where(earlier, 1, 0), axis=0, keepdims=True)
    return ids_row * cap + rank


def dispatch_kernel(cfg, pos_ref, ids_ref, tok_ref, *outs):
    z = pos_ref[0]
    keys = slot_keys(ids_ref[...], cfg.cap)
    keys = jnp.concatenate([keys + j * BIG for j in range(cfg.nd)], axis=1)
    stacked = jnp.concatenate([tok_ref[:, j * cfg.w:(j + 1) * cfg.w] for j in range(cfg.nd)], axis=0)
    i = iota((cfg.rp, 1), 0)
    j = div(i, cfg.rows)
    target = i - j * cfg.rows + j * BIG
    bases = [jnp.bitwise_xor(z, r) * cfg.local * cfg.cap for r in range(cfg.groups)]
    picks = jnp.concatenate([onehot(keys - base == target) for base in bases], axis=0)
    picked = dot(picks, stacked).astype(BF16)
    for r in range(cfg.groups):
        outs[r][...] = picked[r * cfg.rp:(r + 1) * cfg.rp]


def place(cfg, srcs, store):
    i, c = iota((cfg.nd * cfg.ne * 16, 1), 0), iota((1, 2 * cfg.rp), 1)
    slot = i & 7
    want = ((i >> 3) & 1) * cfg.rp + (i >> 4) * cfg.cap + slot
    spread = onehot((want == c) & (slot < cfg.cap))
    for k in range(len(srcs) // 2):
        pair = jnp.concatenate([srcs[2 * k][...], srcs[2 * k + 1][...]], axis=0)
        spaced = dot(spread, pair).astype(BF16)
        for j in range(cfg.nd):
            for e in range(cfg.ne):
                at = (j * cfg.ne + e) * 16
                store(e, k, j, spaced[at:at + 16])


def near_kernel(cfg, pos_ref, *refs):
    ids_ref, route_ref, rows, info = refs[-4:]
    info[0:1] = slot_keys(ids_ref[...], cfg.cap).astype(F32)
    info[1:2] = route_ref[...]

    def store(e, k, j, v):
        rows[e, k * 16:(k + 1) * 16, j * cfg.w:(j + 1) * cfg.w] = v

    place(cfg, refs[:cfg.early * 4], store)


def hidden_rows(cfg, pos_ref, near, far, gate, up, out_ref, first):
    per = cfg.sources * cfg.cap
    i = iota((per, 1), 0)
    s = div(i, cfg.cap)
    slot = i - s * cfg.cap
    rel = jnp.bitwise_xor(s & 3, pos_ref[1] * 2 + pos_ref[2])
    for k, r in enumerate(cfg.visits):
        rel = rel + jnp.where((s >> 2) == r, 4 * k, 0)
    compact = onehot(iota((1, cfg.sources * 8), 1) == rel * 8 + slot)
    for k in range(cfg.ne // 2):
        e = first + k
        x = jnp.concatenate([near[e], far[k]], axis=0)
        both = dot(x, jnp.concatenate([gate[e], up[e]], axis=1))
        g, u = jnp.split(both, 2, axis=1)
        hid = (g / (1.0 + jnp.exp(-g)) * u).astype(BF16)
        out_ref[k * per:(k + 1) * per] = dot(compact, hid).astype(BF16)


def hidden_first_kernel(cfg, pos_ref, *refs):
    late = cfg.sources - cfg.early * 4
    near, gate, up, out_ref, later, now = refs[late:]

    def store(e, k, j, v):
        ref = now if e < cfg.ne // 2 else later
        ref[e % (cfg.ne // 2), k * 16:(k + 1) * 16, j * cfg.w:(j + 1) * cfg.w] = v

    place(cfg, refs[:late], store)
    hidden_rows(cfg, pos_ref, near, now, gate, up, out_ref, 0)


def hidden_second_kernel(cfg, pos_ref, near, far, gate, up, out_ref):
    hidden_rows(cfg, pos_ref, near, far, gate, up, out_ref, cfg.ne // 2)


def down_rows(cfg, pos_ref, parts, down, full, out, first):
    c, t = pos_ref[1], pos_ref[2]
    f = parts[0].shape[1]
    for ref, dc, dt in zip(parts, (0, 1, 0, 1), (0, 0, 1, 1)):
        at = (jnp.bitwise_xor(c, dc) * 2 + jnp.bitwise_xor(t, dt)) * f
        full[:, pl.ds(pl.multiple_of(at, 128), f)] = ref[...]
    per = cfg.sources * cfg.cap
    for k in range(cfg.ne // 2):
        out[k * per:(k + 1) * per] = dot(full[k * per:(k + 1) * per], down[first + k]).astype(BF16)


def sort_rows(cfg, pos_ref, halves, outs):
    per = cfg.sources * cfg.cap
    width = halves[0].shape[1] // 2
    stacked = jnp.concatenate([v[:, q * width:(q + 1) * width] for q in range(2) for v in halves], axis=0)
    m = iota((4 * cfg.rows, 1), 0)
    qt = div(m, cfg.rows)
    p = m - qt * cfg.rows
    e = div(p, cfg.cap)
    slot = p - e * cfg.cap
    want = (qt >> 1) * (cfg.ne * per) + e * per + (qt & 1) * cfg.cap + slot
    lane = iota((1, 2 * cfg.ne * per), 1)
    picks = []
    for k in range(len(outs)):
        r, dc = divmod(k, 2)
        picks.append(onehot(lane - (r * 2 + jnp.bitwise_xor(pos_ref[1], dc)) * 2 * cfg.cap == want))
    sorted_rows = dot(jnp.concatenate(picks, axis=0), stacked).astype(BF16)
    for k, out in enumerate(outs):
        out[...] = sorted_rows[k * 4 * cfg.rows:(k + 1) * 4 * cfg.rows]


def down_first_kernel(cfg, pos_ref, own, x, core, xcore, down, info, out, full):
    down_rows(cfg, pos_ref, (own, x, core, xcore), down, full, out, 0)


def down_second_kernel(cfg, pos_ref, own, x, core, xcore, down, before, *refs):
    outs, full, out = refs[:-2], refs[-2], refs[-1]
    down_rows(cfg, pos_ref, (own, x, core, xcore), down, full, out, cfg.ne // 2)
    sort_rows(cfg, pos_ref, (before, out), outs)


def combine_kernel(cfg, pos_ref, info_own, info_peer, *refs):
    msgs, (mine, other) = refs[:-2], refs[-2:]
    z, c, t = pos_ref[0], pos_ref[1], pos_ref[2]
    block = 4 * cfg.rows
    lanes = iota((1, cfg.groups * block), 1)
    r = div(lanes, block)
    m = lanes - r * block
    qt = div(m, cfg.rows)
    code = jnp.bitwise_xor(r, z) * cfg.local * cfg.cap + m - qt * cfg.rows + qt * BIG
    picks, weights = [], []
    for rel, info in enumerate((info_own, info_peer)):
        key = as_column(info[0:1]).astype(I32)
        weights.append(as_column(info[1:2]))
        picks += [onehot(key + (q * 2 + jnp.bitwise_xor(t, rel)) * BIG == code) for q in range(2)]
    picks = jnp.concatenate(picks, axis=0)
    n = info_own.shape[1]
    for dc in range(2):
        stacked = jnp.concatenate([msgs[k * 2 + dc][...] for k in range(cfg.groups)], axis=0)
        got = dot(picks, stacked)
        width = got.shape[1]
        at = jnp.bitwise_xor(c, dc) * (2 * width)
        for rel, out in enumerate((mine, other)):
            for q in range(2):
                k = rel * 2 + q
                out[:, pl.ds(pl.multiple_of(at + q * width, 128), width)] = (weights[rel] * got[k * n:(k + 1) * n]).astype(BF16)


class Sizes:
    pass


def swap(x, axis):
    return lax.ppermute(x, axis, [(0, 1), (1, 0)])


def on_device(tokens, expert_ids, route_weights, gate_weight, up_weight, down_weight):
    cfg = Sizes()
    n, width = tokens.shape
    cfg.groups = lax.axis_size("expert")
    cfg.local = gate_weight.shape[0]
    experts = cfg.groups * cfg.local
    cfg.cap = max(2, n * 5 // (4 * experts))
    cfg.ne = cfg.local
    cfg.rows = cfg.ne * cfg.cap
    cfg.nd = 16 // cfg.ne
    cfg.w = width // cfg.nd
    cfg.rp = cfg.rows * cfg.nd
    cfg.sources = cfg.groups * 4
    cfg.early = 3
    cfg.visits = (0, 1, 3, 2)
    f = gate_weight.shape[2]
    ff, wide = down_weight.shape[1:]
    per = cfg.sources * cfg.cap

    z, c, t = (lax.axis_index(a) for a in ("expert", "context", "tensor"))
    pos = jnp.stack([z, c, t]).astype(I32)
    ids = expert_ids.reshape(1, n)
    route = route_weights.reshape(1, n)
    smem = pl.BlockSpec(memory_space=pltpu.SMEM)
    vmem = pl.BlockSpec(memory_space=pltpu.VMEM)
    params = pltpu.CompilerParams(vmem_limit_bytes=VMEM_LIMIT)
    shape = jax.ShapeDtypeStruct

    def call(kernel, name, ins, outs, scratch=(), work=10**9):
        args = [pos] + list(ins)
        return list(pl.pallas_call(
            kernel, in_specs=[smem] + [vmem] * len(ins), out_specs=[vmem] * len(outs),
            out_shape=[o if isinstance(o, shape) else shape(o, BF16) for o in outs], scratch_shapes=scratch, compiler_params=params, name=name,
            cost_estimate=pl.CostEstimate(flops=work, bytes_accessed=0, transcendentals=0))(*args))

    def kernel(f):
        return functools.partial(f, cfg)

    blocks = call(kernel(dispatch_kernel), "dispatch", [ids, tokens], [(cfg.rp, cfg.w)] * cfg.groups, work=LEAD)

    def move(x, r, dc):
        return lax.ppermute(x, ("expert", "context"), [
            (i * 2 + k, (i ^ r) * 2 + (k ^ dc)) for i in range(cfg.groups) for k in range(2)])

    half = cfg.ne // 2
    early, late = cfg.early * 32, (cfg.groups - cfg.early) * 32
    held = [blocks[0]] + [move(blocks[r], r, 0) for r in range(1, cfg.groups)]
    crossed = [swap(x, "context") for x in held]


    def four(r):
        return [held[r], swap(held[r], "tensor"), crossed[r], swap(crossed[r], "tensor")]

    near, info = call(kernel(near_kernel), "near", [b for r in cfg.visits[:cfg.early] for b in four(r)] + [ids, route],
                      [(cfg.ne, early, width), shape((2, n), F32)])
    info_peer = swap(info, "tensor")
    far = [b for r in cfg.visits[cfg.early:] for b in four(r)]
    hid_a, later = call(kernel(hidden_first_kernel), "hidden_a", far + [near, gate_weight, up_weight],
                        [(half * per, f), (half, late, width)], [pltpu.VMEM((half, late, width), BF16)], work=STEP)
    xa = swap(hid_a, "context")
    hid_b = call(kernel(hidden_second_kernel), "hidden_b", [near, later, gate_weight, up_weight],
                 [(half * per, f)], work=STEP)[0]
    xb = swap(hid_b, "context")
    full = pltpu.VMEM((half * per, ff), BF16)
    out_a = call(kernel(down_first_kernel), "down_a", [hid_a, xa, swap(hid_a, "tensor"), swap(xa, "tensor"), down_weight, info_peer],
                 [(half * per, wide)], [full], work=STEP)[0]
    message = (4 * cfg.rows, wide // 2)
    outs = call(
        kernel(down_second_kernel), "down_b",
        [hid_b, xb, swap(hid_b, "tensor"), swap(xb, "tensor"), down_weight, out_a],
        [message] * (cfg.groups * 2), [full, pltpu.VMEM((half * per, wide), BF16)], work=STEP)
    returned = [outs[0]] + [move(o, k // 2, k % 2) for k, o in enumerate(outs) if k]
    order = ORDER
    mine, other = call(
        lambda pos_ref, own, peer, *refs: combine_kernel(
            cfg, pos_ref, own, peer, *[refs[order.index(k)] for k in range(len(order))], *refs[len(order):]),
        "combine", [info, info_peer] + [returned[k] for k in order], [(n, 2 * wide)] * 2)
    received = swap(other, "tensor")
    first, second = jnp.where(t == 0, mine, received), jnp.where(t == 0, received, mine)
    return jnp.concatenate([first[:, :wide], second[:, :wide], first[:, wide:], second[:, wide:]], axis=1)


def by_gathers(tokens, expert_ids, route_weights, gate_weight, up_weight, down_weight):
    n, width = tokens.shape
    local = gate_weight.shape[0]
    groups = lax.axis_size("expert")
    experts = local * groups
    cap = max(2, n * 5 // (4 * experts))
    ids = expert_ids[:, 0]
    member = (ids[:, None] == jnp.arange(experts, dtype=I32)[None, :]).astype(I32)
    rank = jnp.sum((jnp.cumsum(member, axis=0) - 1) * member, axis=1)
    key = ids * cap + rank
    pick = onehot(key[:, None] == jnp.arange(experts * cap, dtype=I32)[None, :])
    out = jnp.dot(pick.T, tokens, preferred_element_type=F32).astype(BF16)
    out = out.reshape(groups, local, cap, width).transpose(1, 0, 2, 3)
    inc = lax.all_to_all(out, "expert", split_axis=1, concat_axis=1, tiled=True)
    inc = inc.reshape(local, groups * cap, width)
    rows = lax.all_gather(inc, ("context", "tensor"), axis=1, tiled=True)
    g = jnp.einsum("end,edf->enf", rows, gate_weight, preferred_element_type=F32)
    u = jnp.einsum("end,edf->enf", rows, up_weight, preferred_element_type=F32)
    hid = (jax.nn.silu(g) * u).astype(BF16)
    hid = lax.all_gather(hid, ("context", "tensor"), axis=2, tiled=True)
    res = jnp.einsum("erf,efd->erd", hid, down_weight, preferred_element_type=F32).astype(BF16)
    back = lax.all_to_all(res, ("context", "tensor"), split_axis=1, concat_axis=2, tiled=True)
    back = back.reshape(local, groups, cap, width)
    back = lax.all_to_all(back, "expert", split_axis=1, concat_axis=1, tiled=True)
    back = back.transpose(1, 0, 2, 3).reshape(experts * cap, width)
    picked = jnp.dot(pick, back, preferred_element_type=F32)
    return (route_weights * picked).astype(BF16)


def solution(mesh):
    size = dict(mesh.shape)
    paired = size["context"] == 2 and size["tensor"] == 2 and size["expert"] == 4
    rows = P(("group", "expert", "context", "tensor"), None)
    weights = P("expert", None, ("context", "tensor"))
    return jax.shard_map(
        on_device if paired else by_gathers,
        mesh=mesh,
        in_specs=(rows, rows, rows, weights, weights, weights),
        out_specs=rows,
        check_vma=False,
    )
```

```python
import functools
import jax
import jax.numpy as jnp
from jax import lax
from jax.experimental import pallas as pl
from jax.experimental.pallas import tpu as pltpu
from jax.sharding import PartitionSpec as P

BIG = 4096
ORDER = (0, 4, 3, 5, 1, 6, 7, 2)
LEAD = 20 * 10**9
STEP = 10 * 10**9
VMEM_LIMIT = 8 * 1024 * 1024
F32, BF16, I32 = jnp.float32, jnp.bfloat16, jnp.int32


def div(x, by):
    return ((x.astype(F32) + 0.5) * (1.0 / by)).astype(I32)


def onehot(cond):
    return jnp.where(cond, 1.0, 0.0).astype(BF16)


def dot(a, b):
    return jnp.dot(a, b, preferred_element_type=F32)


def iota(shape, dim):
    return lax.broadcasted_iota(I32, shape, dim)


def as_column(row):
    n = row.shape[1]
    square = jnp.broadcast_to(row, (n, n))
    return jnp.sum(jnp.where(iota((n, n), 0) == iota((n, n), 1), square, jnp.zeros((), row.dtype)), axis=1, keepdims=True)


def slot_keys(ids_row, cap):
    n = ids_row.shape[1]
    ids_col = as_column(ids_row)
    earlier = (ids_col == ids_row) & (iota((n, n), 0) < iota((n, n), 1))
    rank = jnp.sum(jnp.where(earlier, 1, 0), axis=0, keepdims=True)
    return ids_row * cap + rank


def dispatch_kernel(cfg, pos_ref, ids_ref, tok_ref, *outs):
    z = pos_ref[0]
    keys = slot_keys(ids_ref[...], cfg.cap)
    keys = jnp.concatenate([keys + j * BIG for j in range(cfg.nd)], axis=1)
    stacked = jnp.concatenate([tok_ref[:, j * cfg.w:(j + 1) * cfg.w] for j in range(cfg.nd)], axis=0)
    i = iota((cfg.rp, 1), 0)
    j = div(i, cfg.rows)
    target = i - j * cfg.rows + j * BIG
    bases = [jnp.bitwise_xor(z, r) * cfg.local * cfg.cap for r in range(cfg.groups)]
    picks = jnp.concatenate([onehot(keys - base == target) for base in bases], axis=0)
    picked = dot(picks, stacked).astype(BF16)
    for r in range(cfg.groups):
        outs[r][...] = picked[r * cfg.rp:(r + 1) * cfg.rp]


def place(cfg, srcs, store):
    i, c = iota((cfg.nd * cfg.ne * 16, 1), 0), iota((1, 2 * cfg.rp), 1)
    slot = i & 7
    want = ((i >> 3) & 1) * cfg.rp + (i >> 4) * cfg.cap + slot
    spread = onehot((want == c) & (slot < cfg.cap))
    for k in range(len(srcs) // 2):
        pair = jnp.concatenate([srcs[2 * k][...], srcs[2 * k + 1][...]], axis=0)
        spaced = dot(spread, pair).astype(BF16)
        for j in range(cfg.nd):
            for e in range(cfg.ne):
                at = (j * cfg.ne + e) * 16
                store(e, k, j, spaced[at:at + 16])


def near_kernel(cfg, pos_ref, *refs):
    ids_ref, route_ref, rows, info = refs[-4:]
    info[0:1] = slot_keys(ids_ref[...], cfg.cap).astype(F32)
    info[1:2] = route_ref[...]

    def store(e, k, j, v):
        rows[e, k * 16:(k + 1) * 16, j * cfg.w:(j + 1) * cfg.w] = v

    place(cfg, refs[:cfg.early * 4], store)


def hidden_rows(cfg, pos_ref, near, far, gate, up, out_ref, first):
    per = cfg.sources * cfg.cap
    i = iota((per, 1), 0)
    s = div(i, cfg.cap)
    slot = i - s * cfg.cap
    rel = jnp.bitwise_xor(s & 3, pos_ref[1] * 2 + pos_ref[2])
    for k, r in enumerate(cfg.visits):
        rel = rel + jnp.where((s >> 2) == r, 4 * k, 0)
    compact = onehot(iota((1, cfg.sources * 8), 1) == rel * 8 + slot)
    found = []
    for k in range(cfg.ne // 2):
        e = first + k
        x = jnp.concatenate([near[e], far[k]], axis=0)
        both = dot(x, jnp.concatenate([gate[e], up[e]], axis=1))
        g, u = jnp.split(both, 2, axis=1)
        found.append((g / (1.0 + jnp.exp(-g)) * u).astype(BF16))
    packed = dot(compact, jnp.concatenate(found, axis=1)).astype(BF16)
    f = out_ref.shape[1]
    for k in range(cfg.ne // 2):
        out_ref[k * per:(k + 1) * per] = packed[:, k * f:(k + 1) * f]


def hidden_first_kernel(cfg, pos_ref, *refs):
    late = cfg.sources - cfg.early * 4
    near, gate, up, out_ref, later, now = refs[late:]

    def store(e, k, j, v):
        ref = now if e < cfg.ne // 2 else later
        ref[e % (cfg.ne // 2), k * 16:(k + 1) * 16, j * cfg.w:(j + 1) * cfg.w] = v

    place(cfg, refs[:late], store)
    hidden_rows(cfg, pos_ref, near, now, gate, up, out_ref, 0)


def hidden_second_kernel(cfg, pos_ref, near, far, gate, up, out_ref):
    hidden_rows(cfg, pos_ref, near, far, gate, up, out_ref, cfg.ne // 2)


def down_rows(cfg, pos_ref, parts, down, full, out, first):
    c, t = pos_ref[1], pos_ref[2]
    f = parts[0].shape[1]
    for ref, dc, dt in zip(parts, (0, 1, 0, 1), (0, 0, 1, 1)):
        at = (jnp.bitwise_xor(c, dc) * 2 + jnp.bitwise_xor(t, dt)) * f
        full[:, pl.ds(pl.multiple_of(at, 128), f)] = ref[...]
    per = cfg.sources * cfg.cap
    for k in range(cfg.ne // 2):
        out[k * per:(k + 1) * per] = dot(full[k * per:(k + 1) * per], down[first + k]).astype(BF16)


def sort_rows(cfg, pos_ref, halves, outs):
    per = cfg.sources * cfg.cap
    width = halves[0].shape[1] // 2
    stacked = jnp.concatenate([v[:, q * width:(q + 1) * width] for q in range(2) for v in halves], axis=0)
    m = iota((4 * cfg.rows, 1), 0)
    qt = div(m, cfg.rows)
    p = m - qt * cfg.rows
    e = div(p, cfg.cap)
    slot = p - e * cfg.cap
    want = (qt >> 1) * (cfg.ne * per) + e * per + (qt & 1) * cfg.cap + slot
    lane = iota((1, 2 * cfg.ne * per), 1)
    picks = []
    for k in range(len(outs)):
        r, dc = divmod(k, 2)
        picks.append(onehot(lane - (r * 2 + jnp.bitwise_xor(pos_ref[1], dc)) * 2 * cfg.cap == want))
    sorted_rows = dot(jnp.concatenate(picks, axis=0), stacked).astype(BF16)
    for k, out in enumerate(outs):
        out[...] = sorted_rows[k * 4 * cfg.rows:(k + 1) * 4 * cfg.rows]


def down_first_kernel(cfg, pos_ref, own, x, core, xcore, down, info, out, full):
    down_rows(cfg, pos_ref, (own, x, core, xcore), down, full, out, 0)


def down_second_kernel(cfg, pos_ref, own, x, core, xcore, down, before, *refs):
    outs, full, out = refs[:-2], refs[-2], refs[-1]
    down_rows(cfg, pos_ref, (own, x, core, xcore), down, full, out, cfg.ne // 2)
    sort_rows(cfg, pos_ref, (before, out), outs)


def combine_kernel(cfg, pos_ref, info_own, info_peer, *refs):
    msgs, (mine, other) = refs[:-2], refs[-2:]
    z, c, t = pos_ref[0], pos_ref[1], pos_ref[2]
    block = 4 * cfg.rows
    lanes = iota((1, cfg.groups * block), 1)
    r = div(lanes, block)
    m = lanes - r * block
    qt = div(m, cfg.rows)
    code = jnp.bitwise_xor(r, z) * cfg.local * cfg.cap + m - qt * cfg.rows + qt * BIG
    picks, weights = [], []
    for rel, info in enumerate((info_own, info_peer)):
        key = as_column(info[0:1]).astype(I32)
        weights.append(as_column(info[1:2]))
        picks += [onehot(key + (q * 2 + jnp.bitwise_xor(t, rel)) * BIG == code) for q in range(2)]
    picks = jnp.concatenate(picks, axis=0)
    n = info_own.shape[1]
    for dc in range(2):
        stacked = jnp.concatenate([msgs[k * 2 + dc][...] for k in range(cfg.groups)], axis=0)
        got = dot(picks, stacked)
        width = got.shape[1]
        at = jnp.bitwise_xor(c, dc) * (2 * width)
        for rel, out in enumerate((mine, other)):
            for q in range(2):
                k = rel * 2 + q
                out[:, pl.ds(pl.multiple_of(at + q * width, 128), width)] = (weights[rel] * got[k * n:(k + 1) * n]).astype(BF16)


class Sizes:
    pass


def swap(x, axis):
    return lax.ppermute(x, axis, [(0, 1), (1, 0)])


def on_device(tokens, expert_ids, route_weights, gate_weight, up_weight, down_weight):
    cfg = Sizes()
    n, width = tokens.shape
    cfg.groups = lax.axis_size("expert")
    cfg.local = gate_weight.shape[0]
    experts = cfg.groups * cfg.local
    cfg.cap = max(2, n * 5 // (4 * experts))
    cfg.ne = cfg.local
    cfg.rows = cfg.ne * cfg.cap
    cfg.nd = 16 // cfg.ne
    cfg.w = width // cfg.nd
    cfg.rp = cfg.rows * cfg.nd
    cfg.sources = cfg.groups * 4
    cfg.early = 3
    cfg.visits = (0, 1, 3, 2)
    f = gate_weight.shape[2]
    ff, wide = down_weight.shape[1:]
    per = cfg.sources * cfg.cap

    z, c, t = (lax.axis_index(a) for a in ("expert", "context", "tensor"))
    pos = jnp.stack([z, c, t]).astype(I32)
    ids = expert_ids.reshape(1, n)
    route = route_weights.reshape(1, n)
    smem = pl.BlockSpec(memory_space=pltpu.SMEM)
    vmem = pl.BlockSpec(memory_space=pltpu.VMEM)
    params = pltpu.CompilerParams(vmem_limit_bytes=VMEM_LIMIT)
    shape = jax.ShapeDtypeStruct

    def call(kernel, name, ins, outs, scratch=(), work=10**9):
        args = [pos] + list(ins)
        return list(pl.pallas_call(
            kernel, in_specs=[smem] + [vmem] * len(ins), out_specs=[vmem] * len(outs),
            out_shape=[o if isinstance(o, shape) else shape(o, BF16) for o in outs], scratch_shapes=scratch, compiler_params=params, name=name,
            cost_estimate=pl.CostEstimate(flops=work, bytes_accessed=0, transcendentals=0))(*args))

    def kernel(f):
        return functools.partial(f, cfg)

    blocks = call(kernel(dispatch_kernel), "dispatch", [ids, tokens], [(cfg.rp, cfg.w)] * cfg.groups, work=LEAD)

    def move(x, r, dc):
        return lax.ppermute(x, ("expert", "context"), [
            (i * 2 + k, (i ^ r) * 2 + (k ^ dc)) for i in range(cfg.groups) for k in range(2)])

    half = cfg.ne // 2
    early, late = cfg.early * 32, (cfg.groups - cfg.early) * 32
    held = [blocks[0]] + [move(blocks[r], r, 0) for r in range(1, cfg.groups)]
    crossed = [swap(x, "context") for x in held]


    def four(r):
        return [held[r], swap(held[r], "tensor"), crossed[r], swap(crossed[r], "tensor")]

    near, info = call(kernel(near_kernel), "near", [b for r in cfg.visits[:cfg.early] for b in four(r)] + [ids, route],
                      [(cfg.ne, early, width), shape((2, n), F32)])
    info_peer = swap(info, "tensor")
    far = [b for r in cfg.visits[cfg.early:] for b in four(r)]
    hid_a, later = call(kernel(hidden_first_kernel), "hidden_a", far + [near, gate_weight, up_weight],
                        [(half * per, f), (half, late, width)], [pltpu.VMEM((half, late, width), BF16)], work=STEP)
    xa = swap(hid_a, "context")
    hid_b = call(kernel(hidden_second_kernel), "hidden_b", [near, later, gate_weight, up_weight],
                 [(half * per, f)], work=STEP)[0]
    xb = swap(hid_b, "context")
    full = pltpu.VMEM((half * per, ff), BF16)
    out_a = call(kernel(down_first_kernel), "down_a", [hid_a, xa, swap(hid_a, "tensor"), swap(xa, "tensor"), down_weight, info_peer],
                 [(half * per, wide)], [full], work=STEP)[0]
    message = (4 * cfg.rows, wide // 2)
    outs = call(
        kernel(down_second_kernel), "down_b",
        [hid_b, xb, swap(hid_b, "tensor"), swap(xb, "tensor"), down_weight, out_a],
        [message] * (cfg.groups * 2), [full, pltpu.VMEM((half * per, wide), BF16)], work=STEP)
    returned = [outs[0]] + [move(o, k // 2, k % 2) for k, o in enumerate(outs) if k]
    order = ORDER
    mine, other = call(
        lambda pos_ref, own, peer, *refs: combine_kernel(
            cfg, pos_ref, own, peer, *[refs[order.index(k)] for k in range(len(order))], *refs[len(order):]),
        "combine", [info, info_peer] + [returned[k] for k in order], [(n, 2 * wide)] * 2)
    received = swap(other, "tensor")
    first, second = jnp.where(t == 0, mine, received), jnp.where(t == 0, received, mine)
    return jnp.concatenate([first[:, :wide], second[:, :wide], first[:, wide:], second[:, wide:]], axis=1)


def by_gathers(tokens, expert_ids, route_weights, gate_weight, up_weight, down_weight):
    n, width = tokens.shape
    local = gate_weight.shape[0]
    groups = lax.axis_size("expert")
    experts = local * groups
    cap = max(2, n * 5 // (4 * experts))
    ids = expert_ids[:, 0]
    member = (ids[:, None] == jnp.arange(experts, dtype=I32)[None, :]).astype(I32)
    rank = jnp.sum((jnp.cumsum(member, axis=0) - 1) * member, axis=1)
    key = ids * cap + rank
    pick = onehot(key[:, None] == jnp.arange(experts * cap, dtype=I32)[None, :])
    out = jnp.dot(pick.T, tokens, preferred_element_type=F32).astype(BF16)
    out = out.reshape(groups, local, cap, width).transpose(1, 0, 2, 3)
    inc = lax.all_to_all(out, "expert", split_axis=1, concat_axis=1, tiled=True)
    inc = inc.reshape(local, groups * cap, width)
    rows = lax.all_gather(inc, ("context", "tensor"), axis=1, tiled=True)
    g = jnp.einsum("end,edf->enf", rows, gate_weight, preferred_element_type=F32)
    u = jnp.einsum("end,edf->enf", rows, up_weight, preferred_element_type=F32)
    hid = (jax.nn.silu(g) * u).astype(BF16)
    hid = lax.all_gather(hid, ("context", "tensor"), axis=2, tiled=True)
    res = jnp.einsum("erf,efd->erd", hid, down_weight, preferred_element_type=F32).astype(BF16)
    back = lax.all_to_all(res, ("context", "tensor"), split_axis=1, concat_axis=2, tiled=True)
    back = back.reshape(local, groups, cap, width)
    back = lax.all_to_all(back, "expert", split_axis=1, concat_axis=1, tiled=True)
    back = back.transpose(1, 0, 2, 3).reshape(experts * cap, width)
    picked = jnp.dot(pick, back, preferred_element_type=F32)
    return (route_weights * picked).astype(BF16)


def solution(mesh):
    size = dict(mesh.shape)
    paired = size["context"] == 2 and size["tensor"] == 2 and size["expert"] == 4
    rows = P(("group", "expert", "context", "tensor"), None)
    weights = P("expert", None, ("context", "tensor"))
    return jax.shard_map(
        on_device if paired else by_gathers,
        mesh=mesh,
        in_specs=(rows, rows, rows, weights, weights, weights),
        out_specs=rows,
        check_vma=False,
    )
```
